32 devices in a mesh: layers: 2 (over y), fa: 4 (over z), fb: 4 (over x, core).
Axes of the slice: x: 2, y: 2, z: 4, core: 2. Of those that a mesh axis runs over, the one named last changes fastest.
Arguments:
- a_acts: bfloat16 [512, 14336], P(('layers', 'fa', 'fb')), parts along dimension 0, may hold values from -60 to 60, as said below
- b_acts: bfloat16 [512, 14336], P(('layers', 'fa', 'fb')), parts along dimension 0, may hold values from -60 to 60, as said below
Outputs:
- correlation: float32 [28672, 14336], P(('layers', 'fa'), 'fb'), parts along dimension 0
The draws below stay inside these ranges and needn't reach their ends.
There are 2 independent parts, one for each index of `layers`. The reference program is written for one: setup_inputs(seed, part) draws one part's arguments, and reference() takes and returns one part's arrays. A program takes and returns all parts, laid end to end along the dimension named above; each array names one. Nothing has to cross between parts.
Inputs may be any that keep to these rules, and one draw needn't show every extreme that they name: `a_acts`: activations with per-feature offsets and scales. `b_acts`: activations with per-feature offsets and scales.
All inputs are finite; a program needn't handle non-finite values.
Results may differ from the reference program's by a relative error of at most 0.004.
Values may be sent and summed in bfloat16 or wider, within the bound.
No kernel may reach another device: no remote copies, remote signals or barrier semaphores. Data moves between devices by JAX's collectives and lax.ppermute only.
A program may use at most 128 MiB of HBM per device.

```python
import jax
import jax.numpy as jnp
from jax import lax

FF = 14336
TOKENS = 256


def shared_parts(key):
    latent = jnp.clip(jax.random.normal(jax.random.fold_in(key, 101), (TOKENS, FF), jnp.float32), -4.0, 4.0)
    order = jax.random.permutation(jax.random.fold_in(key, 102), FF)
    return (latent, order)


def column_terms(key):
    scale = jnp.exp(jax.random.uniform(jax.random.fold_in(key, 11), (FF,), jnp.float32, 0.0, 2.302585))
    offset = jax.random.uniform(jax.random.fold_in(key, 12), (FF,), jnp.float32, -3.0, 3.0)
    return (scale, offset)


def draw_a_acts(key, part):
    latent, order = shared_parts(key)
    key = jax.random.fold_in(key, 1)
    scale, offset = column_terms(key)
    base = latent
    return (offset + scale * base).astype(jnp.bfloat16)


def draw_b_acts(key, part):
    latent, order = shared_parts(key)
    key = jax.random.fold_in(key, 2)
    scale, offset = column_terms(key)
    noise = jnp.clip(jax.random.normal(jax.random.fold_in(key, 13), (TOKENS, FF), jnp.float32), -4.0, 4.0)
    base = 0.8 * latent[:, order] + 0.6 * noise
    return (offset + scale * base).astype(jnp.bfloat16)


def setup_inputs(seed: int = 0, part: int = 0) -> dict:
    arg_keys = jax.random.split(jax.random.key(seed), 3)
    part_keys = jax.random.split(jax.random.fold_in(arg_keys[2], part), 3)
    return {
        "a_acts": draw_a_acts(jax.random.fold_in(jax.random.fold_in(arg_keys[2], part), 71), part),
        "b_acts": draw_b_acts(jax.random.fold_in(jax.random.fold_in(arg_keys[2], part), 71), part),
    }


def standardize(acts):
    values = acts.astype(jnp.float32)
    mean = lax.optimization_barrier(jnp.mean(values, axis=0))
    centred = values - mean
    var = lax.optimization_barrier(jnp.mean(centred * centred, axis=0))
    return (centred * lax.rsqrt(var + 1e-05)).astype(jnp.bfloat16)

def reference(a_acts, b_acts):
    std_a = standardize(a_acts)
    std_b = standardize(b_acts)
    product = jnp.dot(std_a.T, std_b, preferred_element_type=jnp.float32)
    return product / TOKENS
```

```python
import functools

import jax
import jax.numpy as jnp
from jax import lax
from jax.experimental import pallas as pl
from jax.experimental.pallas import tpu as pltpu
from jax.sharding import PartitionSpec as P

EPS = 1e-05
VMEM = 48 * 1024 * 1024


def block_of(size, limit):
    tiles = size // 128
    best = 1
    for count in range(1, tiles + 1):
        if tiles % count == 0 and count * 128 <= limit:
            best = count
    return best * 128


def chunks_of(size, limit):
    tiles = size // 128
    return max(count for count in range(1, limit + 1) if tiles % count == 0)


def standardize(values):
    count = values.shape[0]
    mean = jnp.sum(values, axis=0, keepdims=True) / count
    centred = values - mean
    var = jnp.sum(centred * centred, axis=0, keepdims=True) / count
    return (centred * lax.rsqrt(var + EPS)).astype(jnp.bfloat16)


def slice_kernel(n_fa, n_fb, a_ref, b_ref, *refs):
    outs, sems = refs[:-1], refs[-1]
    width_a = a_ref.shape[1] // n_fa
    width_b = b_ref.shape[1] // n_fb
    fa = lax.axis_index("fa")
    fb = lax.axis_index("fb")
    copies = []
    for step in range(n_fa):
        start = pl.multiple_of(lax.rem(fa + step, n_fa) * width_a, 128)
        copies.append((a_ref.at[:, pl.ds(start, width_a)], outs[step]))
    for step in range(n_fb):
        start = pl.multiple_of(lax.rem(fb + step, n_fb) * width_b, 128)
        copies.append((b_ref.at[:, pl.ds(start, width_b)], outs[n_fa + step]))
    started = []
    for place, (src, dst) in enumerate(copies):
        copy = pltpu.make_async_copy(src, dst, sems.at[place])
        copy.start()
        started.append(copy)
    for copy in started:
        copy.wait()


def cut_panels(a_acts, b_acts, n_fa, n_fb):
    tok, width_a = a_acts.shape[0], a_acts.shape[1] // n_fa
    width_b = b_acts.shape[1] // n_fb
    shapes = [jax.ShapeDtypeStruct((tok, width_a), a_acts.dtype)] * n_fa
    shapes += [jax.ShapeDtypeStruct((tok, width_b), b_acts.dtype)] * n_fb
    outs = pl.pallas_call(
        functools.partial(slice_kernel, n_fa, n_fb),
        out_shape=shapes,
        in_specs=[pl.BlockSpec(memory_space=pl.ANY)] * 2,
        out_specs=[pl.BlockSpec(memory_space=pl.ANY)] * len(shapes),
        scratch_shapes=[pltpu.SemaphoreType.DMA((len(shapes),))],
        name="cut_panels",
    )(a_acts, b_acts)
    return outs[:n_fa], outs[n_fa:]


def standardize_a_kernel(*refs):
    groups, out = refs[:-1], refs[-1]
    values = jnp.concatenate([ref[...].astype(jnp.float32) for ref in groups], axis=0)
    out[...] = standardize(values).T


def standardize_a(groups):
    rows, width = groups[0].shape
    block = block_of(width, 512)
    total = rows * len(groups)
    return pl.pallas_call(
        standardize_a_kernel,
        out_shape=jax.ShapeDtypeStruct((width, total), jnp.bfloat16),
        grid=(width // block,),
        in_specs=[pl.BlockSpec((rows, block), lambda i: (0, i))] * len(groups),
        out_specs=pl.BlockSpec((block, total), lambda i: (i, 0)),
        compiler_params=pltpu.CompilerParams(vmem_limit_bytes=VMEM),
        cost_estimate=pl.CostEstimate(
            flops=10 * width * total, bytes_accessed=4 * width * total, transcendentals=0
        ),
        name="standardize_a",
    )(*groups)


def product_kernel(n_fa, n_fb, aliased, a_ref, *refs):
    groups = refs[:n_fa]
    out, std = refs[-2], refs[-1]
    tok = groups[0].shape[0] // n_fb

    @pl.when(pl.program_id(0) == 0)
    def _():
        pieces = []
        for j in range(n_fb):
            for i in range(n_fa):
                pieces.append(groups[i][pl.ds(j * tok, tok), :].astype(jnp.float32))
        std[...] = standardize(jnp.concatenate(pieces, axis=0))

    product = jnp.dot(a_ref[...], std[...], preferred_element_type=jnp.float32)
    out[...] = product / std.shape[0]


def product_chunk(std_a, groups, n_fa, n_fb, chunk, n_chunks, buffer):
    height, total = std_a.shape
    rows, width = groups[0].shape
    block = block_of(height, 512)
    in_specs = [pl.BlockSpec((block, total), lambda i: (i, 0))]
    in_specs += [pl.BlockSpec((rows, width), lambda i: (0, 0))] * n_fa
    args = [std_a, *groups]
    aliases = {}
    if buffer is not None:
        aliases = {len(args): 0}
        in_specs.append(pl.BlockSpec(memory_space=pl.ANY))
        args.append(buffer)
    return pl.pallas_call(
        functools.partial(product_kernel, n_fa, n_fb, buffer is not None),
        out_shape=jax.ShapeDtypeStruct((height, width * n_chunks), jnp.float32),
        grid=(height // block,),
        in_specs=in_specs,
        out_specs=pl.BlockSpec((block, width), lambda i: (i, chunk)),
        scratch_shapes=[pltpu.VMEM((total, width), jnp.bfloat16)],
        input_output_aliases=aliases,
        compiler_params=pltpu.CompilerParams(vmem_limit_bytes=VMEM),
        cost_estimate=pl.CostEstimate(
            flops=2 * height * width * total, bytes_accessed=4 * height * width, transcendentals=0
        ),
        name="product_chunk",
    )(*args)


def shifted(x, axis, step):
    size = lax.axis_size(axis)
    return lax.ppermute(x, axis, [(i, (i + step) % size) for i in range(size)])


def per_device(a_acts, b_acts):
    n_fa = lax.axis_size("fa")
    n_fb = lax.axis_size("fb")
    panels_a, panels_b = cut_panels(a_acts, b_acts, n_fa, n_fb)
    own_a = [panels_a[0]] + [shifted(panels_a[s], "fa", s) for s in range(1, n_fa)]
    own_b = [panels_b[0]] + [shifted(panels_b[s], "fb", s) for s in range(1, n_fb)]
    group_a = jnp.concatenate(own_a, axis=0)
    group_b = jnp.concatenate(own_b, axis=0)
    width = group_b.shape[1]
    n_chunks = chunks_of(width, 4)
    step = width // n_chunks
    all_a = [group_a] + [shifted(group_a, "fb", s) for s in range(1, n_fb)]
    std_a = standardize_a(all_a)
    buffer = None
    for chunk in range(n_chunks):
        part = group_b[:, chunk * step : (chunk + 1) * step]
        groups = [part] + [shifted(part, "fa", s) for s in range(1, n_fa)]
        buffer = product_chunk(std_a, groups, n_fa, n_fb, chunk, n_chunks, buffer)
    return buffer


def solution(mesh):
    placed = (P(("layers", "fa", "fb"), None), P(("layers", "fa", "fb"), None))
    return jax.shard_map(
        per_device, mesh=mesh, in_specs=placed, out_specs=P(("layers", "fa"), "fb"), check_vma=False
    )
```

```python
import functools

import jax
import jax.numpy as jnp
from jax import lax
from jax.experimental import pallas as pl
from jax.experimental.pallas import tpu as pltpu
from jax.sharding import PartitionSpec as P

EPS = 1e-05
VMEM = 48 * 1024 * 1024


def block_of(size, limit):
    tiles = size // 128
    best = 1
    for count in range(1, tiles + 1):
        if tiles % count == 0 and count * 128 <= limit:
            best = count
    return best * 128


def chunks_of(size, limit):
    tiles = size // 128
    return max(count for count in range(1, limit + 1) if tiles % count == 0)


def over_count(values, count):
    if count & (count - 1) == 0:
        return values * (1.0 / count)
    return values / count


def standardize(values):
    count = values.shape[0]
    mean = over_count(jnp.sum(values, axis=0, keepdims=True), count)
    centred = values - mean
    var = over_count(jnp.sum(centred * centred, axis=0, keepdims=True), count)
    return (centred * lax.rsqrt(var + EPS)).astype(jnp.bfloat16)


def cut_kernel(n_fa, n_fb, a_ref, b_ref, a_out, b_out):
    tok = a_ref.shape[0]
    width_a, width_b = a_out.shape[1], b_out.shape[1]
    for i in range(n_fa):
        a_out[pl.ds(i * tok, tok), :] = a_ref[:, pl.ds(i * width_a, width_a)]
    for j in range(n_fb):
        b_out[pl.ds(j * tok, tok), :] = b_ref[:, pl.ds(j * width_b, width_b)]


def cut_panels(a_acts, b_acts, n_fa, n_fb):
    tok, width = a_acts.shape
    return pl.pallas_call(
        functools.partial(cut_kernel, n_fa, n_fb),
        out_shape=[
            jax.ShapeDtypeStruct((tok * n_fa, width // n_fa), a_acts.dtype),
            jax.ShapeDtypeStruct((tok * n_fb, width // n_fb), b_acts.dtype),
        ],
        compiler_params=pltpu.CompilerParams(vmem_limit_bytes=VMEM),
        name="cut_panels",
    )(a_acts, b_acts)


def standardize_a_kernel(n_fa, n_fb, *refs):
    groups, out, rows = refs[:n_fb], refs[-2], refs[-1]
    tok = groups[0].shape[0] // n_fa
    fb = lax.axis_index("fb")
    for step, (even, odd) in enumerate(zip(groups[0::2], groups[1::2])):
        for core, ref in enumerate((even, odd)):
            source = lax.rem(fb + n_fb - 2 * step, n_fb)
            if core:
                source = source + 1 - 2 * lax.rem(source, 2)
            for i in range(n_fa):
                place = pl.multiple_of((source + i * n_fb) * tok, tok)
                rows[pl.ds(place, tok), :] = ref[pl.ds(i * tok, tok), :].astype(jnp.float32)
    out[...] = standardize(rows[...]).T


def standardize_a(groups, n_fa, n_fb):
    rows, width = groups[0].shape
    block = block_of(width, 512)
    total = rows * n_fb
    return pl.pallas_call(
        functools.partial(standardize_a_kernel, n_fa, n_fb),
        out_shape=jax.ShapeDtypeStruct((width, total), jnp.bfloat16),
        grid=(width // block,),
        in_specs=[pl.BlockSpec((rows, block), lambda i: (0, i))] * n_fb,
        out_specs=pl.BlockSpec((block, total), lambda i: (i, 0)),
        scratch_shapes=[pltpu.VMEM((total, block), jnp.float32)],
        compiler_params=pltpu.CompilerParams(vmem_limit_bytes=VMEM),
        cost_estimate=pl.CostEstimate(
            flops=10 * width * total, bytes_accessed=4 * width * total, transcendentals=0
        ),
        name="standardize_a",
    )(*groups)


def product_kernel(n_fa, a_ref, *refs):
    groups = refs[:n_fa]
    out, rows, std = refs[-3], refs[-2], refs[-1]
    size = groups[0].shape[0]
    total = std.shape[0]

    @pl.when(pl.program_id(0) == 0)
    def _():
        fa = lax.axis_index("fa")
        for step in range(n_fa):
            place = pl.multiple_of(lax.rem(fa + n_fa - step, n_fa) * size, size)
            rows[pl.ds(place, size), :] = groups[step][...].astype(jnp.float32)
        std[...] = standardize(rows[...])

    product = jnp.dot(a_ref[...], std[...], preferred_element_type=jnp.float32)
    out[...] = over_count(product, total)


def product_chunk(std_a, groups, n_fa, chunk, n_chunks, buffer):
    height, total = std_a.shape
    rows, width = groups[0].shape
    block = block_of(height, 512)
    in_specs = [pl.BlockSpec((block, total), lambda i: (i, 0))]
    in_specs += [pl.BlockSpec((rows, width), lambda i: (0, 0))] * n_fa
    args = [std_a, *groups]
    aliases = {}
    if buffer is not None:
        aliases = {len(args): 0}
        in_specs.append(pl.BlockSpec(memory_space=pl.ANY))
        args.append(buffer)
    return pl.pallas_call(
        functools.partial(product_kernel, n_fa),
        out_shape=jax.ShapeDtypeStruct((height, width * n_chunks), jnp.float32),
        grid=(height // block,),
        in_specs=in_specs,
        out_specs=pl.BlockSpec((block, width), lambda i: (i, chunk)),
        scratch_shapes=[pltpu.VMEM((total, width), jnp.float32), pltpu.VMEM((total, width), jnp.bfloat16)],
        input_output_aliases=aliases,
        compiler_params=pltpu.CompilerParams(vmem_limit_bytes=VMEM),
        cost_estimate=pl.CostEstimate(
            flops=2 * height * width * total, bytes_accessed=4 * height * width, transcendentals=0
        ),
        name="product_chunk",
    )(*args)


def shifted(x, axis, step):
    size = lax.axis_size(axis)
    return lax.ppermute(x, axis, [(i, (i + step) % size) for i in range(size)])


def swapped(x, axis):
    return lax.ppermute(x, axis, [(i, i ^ 1) for i in range(lax.axis_size(axis))])


def per_device(a_acts, b_acts):
    n_fa = lax.axis_size("fa")
    n_fb = lax.axis_size("fb")
    panels_a, panels_b = cut_panels(a_acts, b_acts, n_fa, n_fb)
    group_a = lax.all_to_all(panels_a, "fa", split_axis=0, concat_axis=0, tiled=True)
    group_b = lax.all_to_all(panels_b, "fb", split_axis=0, concat_axis=0, tiled=True)
    width = group_b.shape[1]
    n_chunks = chunks_of(width, 4)
    step = width // n_chunks
    same_core = [group_a] + [shifted(group_a, "fb", 2 * s) for s in range(1, n_fb // 2)]
    all_a = []
    for block in same_core:
        all_a += [block, swapped(block, "fb")]
    std_a = standardize_a(all_a, n_fa, n_fb)
    buffer = None
    for chunk in range(n_chunks):
        part = group_b[:, chunk * step : (chunk + 1) * step]
        groups = [part] + [shifted(part, "fa", s) for s in range(1, n_fa)]
        buffer = product_chunk(std_a, groups, n_fa, chunk, n_chunks, buffer)
    return buffer


def solution(mesh):
    placed = (P(("layers", "fa", "fb"), None), P(("layers", "fa", "fb"), None))
    return jax.shard_map(
        per_device, mesh=mesh, in_specs=placed, out_specs=P(("layers", "fa"), "fb"), check_vma=False
    )
```

```python
import functools

import jax
import jax.numpy as jnp
from jax import lax
from jax.experimental import pallas as pl
from jax.experimental.pallas import tpu as pltpu
from jax.sharding import PartitionSpec as P

EPS = 1e-05
VMEM = 48 * 1024 * 1024


def block_of(size, limit):
    tiles = size // 128
    best = 1
    for count in range(1, tiles + 1):
        if tiles % count == 0 and count * 128 <= limit:
            best = count
    return best * 128


def chunk_widths(width, shares):
    unit = 256 if width % 256 == 0 else 128
    tiles = width // unit
    ends = [round(tiles * sum(shares[: k + 1]) / sum(shares)) for k in range(len(shares))]
    counts = [end - start for start, end in zip([0] + ends, ends)]
    return [count * unit for count in counts if count > 0]


def over_count(values, count):
    if count & (count - 1) == 0:
        return values * (1.0 / count)
    return values / count


def standardize(values):
    count = values.shape[0]
    mean = over_count(jnp.sum(values, axis=0, keepdims=True), count)
    centred = values - mean
    var = over_count(jnp.sum(centred * centred, axis=0, keepdims=True), count)
    return (centred * lax.rsqrt(var + EPS)).astype(jnp.bfloat16)


def cut_kernel(n_fa, n_fb, a_ref, b_ref, *refs):
    outs, sems = refs[:-1], refs[-1]
    width_a = a_ref.shape[1] // n_fa
    width_b = b_ref.shape[1] // n_fb
    fa = lax.axis_index("fa")
    fb = lax.axis_index("fb")
    copies = []
    for step in range(n_fa):
        start = pl.multiple_of(lax.rem(fa + step, n_fa) * width_a, 128)
        copies.append((a_ref.at[:, pl.ds(start, width_a)], outs[step]))
    for step in range(n_fb):
        start = pl.multiple_of(lax.rem(fb + step, n_fb) * width_b, 128)
        copies.append((b_ref.at[:, pl.ds(start, width_b)], outs[n_fa + step]))
    started = []
    for place, (src, dst) in enumerate(copies):
        copy = pltpu.make_async_copy(src, dst, sems.at[place])
        copy.start()
        started.append(copy)
    for copy in started:
        copy.wait()


def cut_panels(a_acts, b_acts, n_fa, n_fb):
    tok, width = a_acts.shape
    shapes = [jax.ShapeDtypeStruct((tok, width // n_fa), a_acts.dtype)] * n_fa
    shapes += [jax.ShapeDtypeStruct((tok, width // n_fb), b_acts.dtype)] * n_fb
    outs = pl.pallas_call(
        functools.partial(cut_kernel, n_fa, n_fb),
        out_shape=shapes,
        in_specs=[pl.BlockSpec(memory_space=pl.ANY)] * 2,
        out_specs=[pl.BlockSpec(memory_space=pltpu.VMEM)] * len(shapes),
        scratch_shapes=[pltpu.SemaphoreType.DMA((len(shapes),))],
        compiler_params=pltpu.CompilerParams(vmem_limit_bytes=VMEM),
        name="cut_panels",
    )(a_acts, b_acts)
    return outs[:n_fa], outs[n_fa:]


def join_kernel(n_in, n_out, *refs):
    tok = refs[0].shape[0]
    column = 0
    for out in refs[-n_out:]:
        width = out.shape[1]
        for i in range(n_in):
            out[pl.ds(i * tok, tok), :] = refs[i][:, pl.ds(column, width)]
        column += width


def join_rows(pieces, widths, after=()):
    rows = pieces[0].shape[0] * len(pieces)
    return pl.pallas_call(
        functools.partial(join_kernel, len(pieces), len(widths)),
        out_shape=[jax.ShapeDtypeStruct((rows, width), pieces[0].dtype) for width in widths],
        in_specs=[pl.BlockSpec(memory_space=pltpu.VMEM)] * len(pieces)
        + [pl.BlockSpec(memory_space=pl.ANY)] * len(after),
        out_specs=[pl.BlockSpec(memory_space=pltpu.VMEM)] * len(widths),
        compiler_params=pltpu.CompilerParams(vmem_limit_bytes=VMEM),
        name="join_rows",
    )(*pieces, *after)


def standardize_a_kernel(n_fa, n_fb, *refs):
    groups, out, rows = refs[:n_fb], refs[-2], refs[-1]
    tok = groups[0].shape[0] // n_fa
    odd = lax.rem(lax.axis_index("fb"), 2)
    for place, ref in enumerate(groups):
        back = place if place % 2 == 0 else lax.rem(place - 2 + 2 * odd + n_fb, n_fb)
        for i in range(n_fa):
            row = (i * n_fb + back) * tok
            if place % 2:
                row = pl.multiple_of(row, tok)
            rows[pl.ds(row, tok), :] = ref[pl.ds(i * tok, tok), :].astype(jnp.float32)
    out[...] = standardize(rows[...]).T


def standardize_a(groups, n_fa, n_fb):
    rows, width = groups[0].shape
    block = block_of(width, 512)
    total = rows * n_fb
    return pl.pallas_call(
        functools.partial(standardize_a_kernel, n_fa, n_fb),
        out_shape=jax.ShapeDtypeStruct((width, total), jnp.bfloat16),
        grid=(width // block,),
        in_specs=[pl.BlockSpec((rows, block), lambda i: (0, i))] * n_fb,
        out_specs=pl.BlockSpec((block, total), lambda i: (i, 0)),
        scratch_shapes=[pltpu.VMEM((total, block), jnp.float32)],
        compiler_params=pltpu.CompilerParams(vmem_limit_bytes=VMEM),
        cost_estimate=pl.CostEstimate(
            flops=10 * width * total, bytes_accessed=4 * width * total, transcendentals=0
        ),
        name="standardize_a",
    )(*groups)


def product_kernel(n_fa, column, a_ref, *refs):
    groups = refs[:n_fa]
    out, std, slots, sems = refs[-4:]
    total, width = std.shape
    n_slots, block = slots.shape[0], slots.shape[1]
    steps = a_ref.shape[0] // block

    @pl.loop(0, width // 128)
    def _(strip):
        columns = pl.ds(pl.multiple_of(strip * 128, 128), 128)
        values = jnp.concatenate([ref[:, columns].astype(jnp.float32) for ref in groups], axis=0)
        std[:, columns] = standardize(values)

    def copy_of(step):
        slot = lax.rem(step, n_slots)
        place = pl.multiple_of(step * block, block)
        return pltpu.make_async_copy(
            slots.at[slot], out.at[pl.ds(place, block), pl.ds(column, width)], sems.at[slot]
        )

    @pl.loop(0, steps)
    def _(step):
        @pl.when(step >= n_slots)
        def _():
            copy_of(step - n_slots).wait()

        place = pl.multiple_of(step * block, block)
        product = jnp.dot(a_ref[pl.ds(place, block), :], std[...], preferred_element_type=jnp.float32)
        slots[lax.rem(step, n_slots)] = over_count(product, total)
        copy_of(step).start()

    @pl.loop(max(steps - n_slots, 0), steps)
    def _(step):
        copy_of(step).wait()


def product_chunk(std_a, groups, column, full_width, buffer):
    height, total = std_a.shape
    width = groups[0].shape[1]
    block = block_of(height, 512)
    in_specs = [pl.BlockSpec(memory_space=pltpu.VMEM)] * (1 + len(groups))
    args = [std_a, *groups]
    aliases = {}
    if buffer is not None:
        aliases = {len(args): 0}
        in_specs.append(pl.BlockSpec(memory_space=pl.ANY))
        args.append(buffer)
    return pl.pallas_call(
        functools.partial(product_kernel, len(groups), column),
        out_shape=jax.ShapeDtypeStruct((height, full_width), jnp.float32),
        in_specs=in_specs,
        out_specs=pl.BlockSpec(memory_space=pl.ANY),
        scratch_shapes=[
            pltpu.VMEM((total, width), jnp.bfloat16),
            pltpu.VMEM((4, block, width), jnp.float32),
            pltpu.SemaphoreType.DMA((4,)),
        ],
        input_output_aliases=aliases,
        compiler_params=pltpu.CompilerParams(vmem_limit_bytes=VMEM),
        cost_estimate=pl.CostEstimate(
            flops=2 * height * width * total, bytes_accessed=4 * height * width, transcendentals=0
        ),
        name="product_chunk",
    )(*args)


def shifted(x, axis, step):
    size = lax.axis_size(axis)
    return lax.ppermute(x, axis, [(i, (i + step) % size) for i in range(size)])


def swapped(x, axis):
    return lax.ppermute(x, axis, [(i, i ^ 1) for i in range(lax.axis_size(axis))])


def per_device(a_acts, b_acts):
    n_fa = lax.axis_size("fa")
    n_fb = lax.axis_size("fb")
    panels_a, panels_b = cut_panels(a_acts, b_acts, n_fa, n_fb)
    own_a = [panels_a[0]] + [shifted(panels_a[s], "fa", s) for s in range(1, n_fa)]
    own_b = [panels_b[0]] + [shifted(panels_b[s], "fb", s) for s in range(1, n_fb)]
    full_width = panels_b[0].shape[1]
    widths = chunk_widths(full_width, (6, 5, 3))
    parts_b = join_rows(own_b, widths)
    group_a = join_rows(own_a, [panels_a[0].shape[1]], parts_b[-1:])[0]
    same_core = [group_a] + [shifted(group_a, "fb", 2 * s) for s in range(1, n_fb // 2)]
    all_a = []
    for block in same_core:
        all_a += [block, swapped(block, "fb")]
    std_a = standardize_a(all_a, n_fa, n_fb)
    buffer = None
    column = 0
    for part in parts_b:
        groups = [part] + [shifted(part, "fa", s) for s in range(1, n_fa)]
        buffer = product_chunk(std_a, groups, column, full_width, buffer)
        column += part.shape[1]
    return buffer


def solution(mesh):
    placed = (P(("layers", "fa", "fb"), None), P(("layers", "fa", "fb"), None))
    return jax.shard_map(
        per_device, mesh=mesh, in_specs=placed, out_specs=P(("layers", "fa"), "fb"), check_vma=False
    )
```

```python
import functools

import jax
import jax.numpy as jnp
from jax import lax
from jax.experimental import pallas as pl
from jax.experimental.pallas import tpu as pltpu
from jax.sharding import PartitionSpec as P

EPS = 1e-05
VMEM = 48 * 1024 * 1024


def block_of(size, limit):
    tiles = size // 128
    best = 1
    for count in range(1, tiles + 1):
        if tiles % count == 0 and count * 128 <= limit:
            best = count
    return best * 128


def chunk_widths(width, shares):
    unit = 256 if width % 256 == 0 else 128
    tiles = width // unit
    ends = [round(tiles * sum(shares[: k + 1]) / sum(shares)) for k in range(len(shares))]
    counts = [end - start for start, end in zip([0] + ends, ends)]
    return [count * unit for count in counts if count > 0]


def over_count(values, count):
    if count & (count - 1) == 0:
        return values * (1.0 / count)
    return values / count


def standardize(values):
    count = values.shape[0]
    mean = over_count(jnp.sum(values, axis=0, keepdims=True), count)
    centred = values - mean
    var = over_count(jnp.sum(centred * centred, axis=0, keepdims=True), count)
    return (centred * lax.rsqrt(var + EPS)).astype(jnp.bfloat16)


def cut_kernel(n_fa, n_fb, a_ref, b_ref, *refs):
    outs, sems = refs[:-1], refs[-1]
    width_a = a_ref.shape[1] // n_fa
    width_b = b_ref.shape[1] // n_fb
    fa = lax.axis_index("fa")
    fb = lax.axis_index("fb")
    copies = []
    for step in range(n_fa):
        start = pl.multiple_of(lax.rem(fa + step, n_fa) * width_a, 128)
        copies.append((a_ref.at[:, pl.ds(start, width_a)], outs[step]))
    for step in range(n_fb):
        start = pl.multiple_of(lax.rem(fb + step, n_fb) * width_b, 128)
        copies.append((b_ref.at[:, pl.ds(start, width_b)], outs[n_fa + step]))
    started = []
    for place, (src, dst) in enumerate(copies):
        copy = pltpu.make_async_copy(src, dst, sems.at[place])
        copy.start()
        started.append(copy)
    for copy in started:
        copy.wait()


def cut_panels(a_acts, b_acts, n_fa, n_fb):
    tok, width = a_acts.shape
    shapes = [jax.ShapeDtypeStruct((tok, width // n_fa), a_acts.dtype)] * n_fa
    shapes += [jax.ShapeDtypeStruct((tok, width // n_fb), b_acts.dtype)] * n_fb
    outs = pl.pallas_call(
        functools.partial(cut_kernel, n_fa, n_fb),
        out_shape=shapes,
        in_specs=[pl.BlockSpec(memory_space=pl.ANY)] * 2,
        out_specs=[pl.BlockSpec(memory_space=pltpu.VMEM)] * len(shapes),
        scratch_shapes=[pltpu.SemaphoreType.DMA((len(shapes),))],
        compiler_params=pltpu.CompilerParams(vmem_limit_bytes=VMEM),
        name="cut_panels",
    )(a_acts, b_acts)
    return outs[:n_fa], outs[n_fa:]


def join_kernel(shapes, *refs):
    n_in = sum(len_in for len_in, _ in shapes)
    n_out = sum(len_out for _, len_out in shapes)
    ins, outs = refs[:n_in], refs[-n_out:]
    for len_in, len_out in shapes:
        tok = ins[0].shape[0]
        column = 0
        for out in outs[:len_out]:
            width = out.shape[1]
            for i in range(len_in):
                out[pl.ds(i * tok, tok), :] = ins[i][:, pl.ds(column, width)]
            column += width
        ins, outs = ins[len_in:], outs[len_out:]


def join_rows(groups, after=()):
    pieces = [piece for group, _ in groups for piece in group]
    shapes = [
        jax.ShapeDtypeStruct((group[0].shape[0] * len(group), width), group[0].dtype)
        for group, widths in groups
        for width in widths
    ]
    return pl.pallas_call(
        functools.partial(join_kernel, [(len(group), len(widths)) for group, widths in groups]),
        out_shape=shapes,
        in_specs=[pl.BlockSpec(memory_space=pltpu.VMEM)] * len(pieces)
        + [pl.BlockSpec(memory_space=pl.ANY)] * len(after),
        out_specs=[pl.BlockSpec(memory_space=pltpu.VMEM)] * len(shapes),
        compiler_params=pltpu.CompilerParams(vmem_limit_bytes=VMEM),
        name="join_rows",
    )(*pieces, *after)


def stacked(pieces, after=()):
    return join_rows([(pieces, [pieces[0].shape[1]])], after)[0]


def order_of(source, fa, n_fa):
    if n_fa != 4:
        return lax.rem(fa + n_fa - source, n_fa)
    neighbour = fa + 1 - 2 * lax.rem(fa, 2)
    outer = jnp.where((source == 0) | (source == n_fa - 1), 3, 2)
    return jnp.where(source == fa, 0, jnp.where(source == neighbour, 1, outer))


def standardize_a_kernel(n_fa, n_fb, *refs):
    groups, out, rows = refs[:n_fb], refs[-2], refs[-1]
    tok = groups[0].shape[0] // n_fa
    fa = lax.axis_index("fa")
    odd = lax.rem(lax.axis_index("fb"), 2)
    places = [order_of(lax.rem(fa + n_fa - i, n_fa), fa, n_fa) for i in range(n_fa)]
    for place, ref in enumerate(groups):
        back = place if place % 2 == 0 else lax.rem(place - 2 + 2 * odd + n_fb, n_fb)
        for i in range(n_fa):
            row = pl.multiple_of((places[i] * n_fb + back) * tok, tok)
            rows[pl.ds(row, tok), :] = ref[pl.ds(i * tok, tok), :].astype(jnp.float32)
    out[...] = standardize(rows[...]).T


def standardize_a(groups, n_fa, n_fb):
    rows, width = groups[0].shape
    block = block_of(width, 512)
    total = rows * n_fb
    return pl.pallas_call(
        functools.partial(standardize_a_kernel, n_fa, n_fb),
        out_shape=jax.ShapeDtypeStruct((width, total), jnp.bfloat16),
        grid=(width // block,),
        in_specs=[pl.BlockSpec((rows, block), lambda i: (0, i))] * n_fb,
        out_specs=pl.BlockSpec((block, total), lambda i: (i, 0)),
        scratch_shapes=[pltpu.VMEM((total, block), jnp.float32)],
        compiler_params=pltpu.CompilerParams(vmem_limit_bytes=VMEM),
        cost_estimate=pl.CostEstimate(
            flops=10 * width * total, bytes_accessed=4 * width * total, transcendentals=0
        ),
        name="standardize_a",
    )(*groups)


def product_kernel(n_groups, relayed, column, a_ref, *refs):
    groups = refs[:n_groups]
    out, std, slots, sems = refs[-4:]
    total, width = std.shape
    n_slots, height, strip = slots.shape
    fa = lax.axis_index("fa")
    at_end = (fa == 0) | (fa == 3)

    def copy_of(step):
        slot = lax.rem(step, n_slots)
        place = pl.multiple_of(column + step * strip, 128)
        return pltpu.make_async_copy(slots.at[slot], out.at[:, pl.ds(place, strip)], sems.at[slot])

    @pl.loop(0, width // 128)
    def _(step):
        columns = pl.ds(pl.multiple_of(step * 128, 128), 128)
        pieces = [ref[:, columns].astype(jnp.float32) for ref in groups]
        if relayed:
            pieces = [pieces[0], jnp.where(at_end, pieces[2], pieces[1])]
        std[:, columns] = standardize(jnp.concatenate(pieces, axis=0))

    @pl.loop(0, width // strip)
    def _(step):
        @pl.when(step >= n_slots)
        def _():
            copy_of(step - n_slots).wait()

        columns = pl.ds(pl.multiple_of(step * strip, 128), strip)
        product = jnp.dot(a_ref[...], std[:, columns], preferred_element_type=jnp.float32)
        slots[lax.rem(step, n_slots)] = over_count(product, total)
        copy_of(step).start()

    @pl.loop(max(width // strip - n_slots, 0), width // strip)
    def _(step):
        copy_of(step).wait()


def product_chunk(std_a, groups, relayed, column, full_width, buffer):
    height, total = std_a.shape
    width = groups[0].shape[1]
    strip = 256 if width % 256 == 0 else 128
    n_slots = 4
    in_specs = [pl.BlockSpec(memory_space=pltpu.VMEM)] * (1 + len(groups))
    args = [std_a, *groups]
    aliases = {}
    if buffer is not None:
        aliases = {len(args): 0}
        in_specs.append(pl.BlockSpec(memory_space=pl.ANY))
        args.append(buffer)
    return pl.pallas_call(
        functools.partial(product_kernel, len(groups), relayed, column),
        out_shape=jax.ShapeDtypeStruct((height, full_width), jnp.float32),
        in_specs=in_specs,
        out_specs=pl.BlockSpec(memory_space=pl.ANY),
        scratch_shapes=[
            pltpu.VMEM((total, width), jnp.bfloat16),
            pltpu.VMEM((n_slots, height, strip), jnp.float32),
            pltpu.SemaphoreType.DMA((n_slots,)),
        ],
        input_output_aliases=aliases,
        compiler_params=pltpu.CompilerParams(vmem_limit_bytes=VMEM),
        cost_estimate=pl.CostEstimate(
            flops=2 * height * width * total, bytes_accessed=4 * height * width, transcendentals=0
        ),
        name="product_chunk",
    )(*args)


def shifted(x, axis, step):
    size = lax.axis_size(axis)
    return lax.ppermute(x, axis, [(i, (i + step) % size) for i in range(size)])


def swapped(x, axis):
    return lax.ppermute(x, axis, [(i, i ^ 1) for i in range(lax.axis_size(axis))])


def per_device(a_acts, b_acts):
    n_fa = lax.axis_size("fa")
    n_fb = lax.axis_size("fb")
    relayed = n_fa == 4
    panels_a, panels_b = cut_panels(a_acts, b_acts, n_fa, n_fb)
    own_a = [panels_a[0]] + [shifted(panels_a[s], "fa", s) for s in range(1, n_fa)]
    own_b = [panels_b[0]] + [shifted(panels_b[s], "fb", s) for s in range(1, n_fb)]
    full_width = panels_b[0].shape[1]
    widths = chunk_widths(full_width, (1, 1))
    group_a, *parts_b = join_rows([(own_a, [panels_a[0].shape[1]]), (own_b, widths)])
    if relayed:
        pairs = []
        for part in parts_b:
            if pairs:
                part = stacked([part], pairs[-1:])
            pairs.append(stacked([part, swapped(part, "fa")]))
        seconds = [lax.ppermute(pair, "fa", [(0, 0), (1, 2), (2, 1), (3, 3)]) for pair in pairs]
        chunks = [[pair, second, swapped(second, "fa")] for pair, second in zip(pairs, seconds)]
        ahead = pairs[:1]
    else:
        chunks = [[part] + [shifted(part, "fa", s) for s in range(1, n_fa)] for part in parts_b]
        ahead = parts_b[:1]
    all_a = [group_a, swapped(group_a, "fb")]
    for s in range(1, n_fb // 2):
        block = shifted(group_a, "fb", 2 * s)
        all_a += [block, swapped(stacked([block], ahead), "fb")]
    std_a = standardize_a(all_a, n_fa, n_fb)
    buffer = None
    column = 0
    for groups in chunks:
        buffer = product_chunk(std_a, groups, relayed, column, full_width, buffer)
        column += groups[0].shape[1]
    return buffer


def solution(mesh):
    placed = (P(("layers", "fa", "fb"), None), P(("layers", "fa", "fb"), None))
    return jax.shard_map(
        per_device, mesh=mesh, in_specs=placed, out_specs=P(("layers", "fa"), "fb"), check_vma=False
    )
```

```python
import functools

import jax
import jax.numpy as jnp
from jax import lax
from jax.experimental import pallas as pl
from jax.experimental.pallas import tpu as pltpu
from jax.sharding import PartitionSpec as P

EPS = 1e-05
VMEM = 48 * 1024 * 1024


def block_of(size, limit):
    tiles = size // 128
    best = 1
    for count in range(1, tiles + 1):
        if tiles % count == 0 and count * 128 <= limit:
            best = count
    return best * 128


def chunk_widths(width, shares):
    unit = 256 if width % 256 == 0 else 128
    tiles = width // unit
    ends = [round(tiles * sum(shares[: k + 1]) / sum(shares)) for k in range(len(shares))]
    counts = [end - start for start, end in zip([0] + ends, ends)]
    return [count * unit for count in counts if count > 0]


def over_count(values, count):
    if power_of_two(count):
        return values * (1.0 / count)
    return values / count


def standardize(values):
    count = values.shape[0]
    mean = over_count(jnp.sum(values, axis=0, keepdims=True), count)
    centred = values - mean
    var = over_count(jnp.sum(centred * centred, axis=0, keepdims=True), count)
    return (centred * lax.rsqrt(var + EPS)).astype(jnp.bfloat16)


def power_of_two(count):
    return count & (count - 1) == 0


def partner(place, step, size):
    if power_of_two(size):
        return place ^ step
    return (place + step) % size


def cut_kernel(n_fa, n_fb, a_ref, b_ref, *refs):
    outs, sems = refs[:-1], refs[-1]
    width_a = a_ref.shape[1] // n_fa
    width_b = b_ref.shape[1] // n_fb
    fa = lax.axis_index("fa")
    fb = lax.axis_index("fb")
    copies = []
    for step in range(n_fa):
        start = pl.multiple_of(partner(fa, step, n_fa) * width_a, 128)
        copies.append((a_ref.at[:, pl.ds(start, width_a)], outs[step]))
    for step in range(n_fb):
        start = pl.multiple_of(partner(fb, step, n_fb) * width_b, 128)
        copies.append((b_ref.at[:, pl.ds(start, width_b)], outs[n_fa + step]))
    started = []
    for place, (src, dst) in enumerate(copies):
        copy = pltpu.make_async_copy(src, dst, sems.at[place])
        copy.start()
        started.append(copy)
    for copy in started:
        copy.wait()


def cut_panels(a_acts, b_acts, n_fa, n_fb):
    tok, width = a_acts.shape
    shapes = [jax.ShapeDtypeStruct((tok, width // n_fa), a_acts.dtype)] * n_fa
    shapes += [jax.ShapeDtypeStruct((tok, width // n_fb), b_acts.dtype)] * n_fb
    outs = pl.pallas_call(
        functools.partial(cut_kernel, n_fa, n_fb),
        out_shape=shapes,
        in_specs=[pl.BlockSpec(memory_space=pl.ANY)] * 2,
        out_specs=[pl.BlockSpec(memory_space=pltpu.VMEM)] * len(shapes),
        scratch_shapes=[pltpu.SemaphoreType.DMA((len(shapes),))],
        compiler_params=pltpu.CompilerParams(vmem_limit_bytes=VMEM),
        name="cut_panels",
    )(a_acts, b_acts)
    return outs[:n_fa], outs[n_fa:]


def join_kernel(shapes, *refs):
    n_in = sum(len_in for len_in, _ in shapes)
    n_out = sum(len_out for _, len_out in shapes)
    ins, outs = refs[:n_in], refs[-n_out:]
    for len_in, len_out in shapes:
        tok = ins[0].shape[0]
        column = 0
        for out in outs[:len_out]:
            width = out.shape[1]
            for i in range(len_in):
                out[pl.ds(i * tok, tok), :] = ins[i][:, pl.ds(column, width)]
            column += width
        ins, outs = ins[len_in:], outs[len_out:]


def join_rows(groups, after=()):
    pieces = [piece for group, _ in groups for piece in group]
    shapes = [
        jax.ShapeDtypeStruct((group[0].shape[0] * len(group), width), group[0].dtype)
        for group, widths in groups
        for width in widths
    ]
    return pl.pallas_call(
        functools.partial(join_kernel, [(len(group), len(widths)) for group, widths in groups]),
        out_shape=shapes,
        in_specs=[pl.BlockSpec(memory_space=pltpu.VMEM)] * len(pieces)
        + [pl.BlockSpec(memory_space=pl.ANY)] * len(after),
        out_specs=[pl.BlockSpec(memory_space=pltpu.VMEM)] * len(shapes),
        compiler_params=pltpu.CompilerParams(vmem_limit_bytes=VMEM),
        name="join_rows",
    )(*pieces, *after)


def stacked(pieces, after=()):
    return join_rows([(pieces, [pieces[0].shape[1]])], after)[0]


def standardize_a_kernel(n_fa, n_fb, *refs):
    groups, out = refs[:n_fb], refs[-1]
    tok = groups[0].shape[0] // n_fa
    pieces = [
        group[pl.ds(i * tok, tok), :].astype(jnp.float32) for i in range(n_fa) for group in groups
    ]
    out[...] = standardize(jnp.concatenate(pieces, axis=0)).T


def standardize_a(groups, n_fa, n_fb):
    rows, width = groups[0].shape
    block = block_of(width, 512)
    total = rows * n_fb
    return pl.pallas_call(
        functools.partial(standardize_a_kernel, n_fa, n_fb),
        out_shape=jax.ShapeDtypeStruct((width, total), jnp.bfloat16),
        grid=(width // block,),
        in_specs=[pl.BlockSpec((rows, block), lambda i: (0, i))] * n_fb,
        out_specs=pl.BlockSpec((block, total), lambda i: (i, 0)),
        compiler_params=pltpu.CompilerParams(vmem_limit_bytes=VMEM),
        cost_estimate=pl.CostEstimate(
            flops=10 * width * total, bytes_accessed=4 * width * total, transcendentals=0
        ),
        name="standardize_a",
    )(*groups)


def product_kernel(n_groups, column, a_ref, *refs):
    groups = refs[:n_groups]
    out, slots, sems = refs[-3:]
    total, width = a_ref.shape[1], groups[0].shape[1]
    n_slots, height, strip = slots.shape

    def copy_of(step):
        slot = lax.rem(step, n_slots)
        place = pl.multiple_of(column + step * strip, 128)
        return pltpu.make_async_copy(slots.at[slot], out.at[:, pl.ds(place, strip)], sems.at[slot])

    @pl.loop(0, width // strip)
    def _(step):
        @pl.when(step >= n_slots)
        def _():
            copy_of(step - n_slots).wait()

        parts = []
        for part in range(strip // 128):
            columns = pl.ds(pl.multiple_of(step * strip + part * 128, 128), 128)
            pieces = [ref[:, columns].astype(jnp.float32) for ref in groups]
            parts.append(standardize(jnp.concatenate(pieces, axis=0)))
        std = jnp.concatenate(parts, axis=1)
        product = jnp.dot(a_ref[...], std, preferred_element_type=jnp.float32)
        slots[lax.rem(step, n_slots)] = over_count(product, total)
        copy_of(step).start()

    @pl.loop(max(width // strip - n_slots, 0), width // strip)
    def _(step):
        copy_of(step).wait()


def product_chunk(std_a, groups, column, full_width, buffer, after=()):
    height, total = std_a.shape
    width = groups[0].shape[1]
    strip = 256 if width % 256 == 0 else 128
    n_slots = 4
    in_specs = [pl.BlockSpec(memory_space=pltpu.VMEM)] * (1 + len(groups))
    in_specs += [pl.BlockSpec(memory_space=pl.ANY)] * len(after)
    args = [std_a, *groups, *after]
    aliases = {}
    if buffer is not None:
        aliases = {len(args): 0}
        in_specs.append(pl.BlockSpec(memory_space=pl.ANY))
        args.append(buffer)
    return pl.pallas_call(
        functools.partial(product_kernel, len(groups), column),
        out_shape=jax.ShapeDtypeStruct((height, full_width), jnp.float32),
        in_specs=in_specs,
        out_specs=pl.BlockSpec(memory_space=pl.ANY),
        scratch_shapes=[
            pltpu.VMEM((n_slots, height, strip), jnp.float32),
            pltpu.SemaphoreType.DMA((n_slots,)),
        ],
        input_output_aliases=aliases,
        compiler_params=pltpu.CompilerParams(vmem_limit_bytes=VMEM),
        cost_estimate=pl.CostEstimate(
            flops=2 * height * width * total, bytes_accessed=4 * height * width, transcendentals=0
        ),
        name="product_chunk",
    )(*args)


def sent(x, axis, step):
    size = lax.axis_size(axis)
    return lax.ppermute(x, axis, [(i, partner(i, step, size)) for i in range(size)])


def gathered(x, axis, through=None):
    size = lax.axis_size(axis)
    blocks = [x]
    for step in range(1, size):
        low = step & -step
        if through is None or low == step or not power_of_two(size):
            blocks.append(sent(x, axis, step))
        else:
            blocks.append(sent(through(blocks[step - low]), axis, low))
    return blocks


def per_device(a_acts, b_acts):
    n_fa = lax.axis_size("fa")
    n_fb = lax.axis_size("fb")
    panels_a, panels_b = cut_panels(a_acts, b_acts, n_fa, n_fb)
    own_a = [panels_a[0]] + [sent(panels_a[s], "fa", s) for s in range(1, n_fa)]
    own_b = [panels_b[0]] + [sent(panels_b[s], "fb", s) for s in range(1, n_fb)]
    full_width = panels_b[0].shape[1]
    widths = chunk_widths(full_width, (4, 5, 5))
    group_a, *parts_b = join_rows([(own_a, [panels_a[0].shape[1]]), (own_b, widths)])
    chunks = [gathered(part, "fa", lambda block: block) for part in parts_b[:-1]]
    chunks.append(gathered(parts_b[-1], "fa"))
    far = n_fa // 2
    all_a = gathered(group_a, "fb", lambda block: stacked([block], [chunks[0][1]] + [chunk[far] for chunk in chunks[:-1]]))
    std_a = standardize_a(all_a, n_fa, n_fb)
    buffer = None
    column = 0
    for place, groups in enumerate(chunks):
        after = [later[far] for later in chunks[place + 1 : -1]]
        buffer = product_chunk(std_a, groups, column, full_width, buffer, after)
        column += groups[0].shape[1]
    return buffer


def solution(mesh):
    placed = (P(("layers", "fa", "fb"), None), P(("layers", "fa", "fb"), None))
    return jax.shard_map(
        per_device, mesh=mesh, in_specs=placed, out_specs=P(("layers", "fa"), "fb"), check_vma=False
    )
```

```python
import functools

import jax
import jax.numpy as jnp
from jax import lax
from jax.experimental import pallas as pl
from jax.experimental.pallas import tpu as pltpu
from jax.sharding import PartitionSpec as P

EPS = 1e-05
VMEM = 48 * 1024 * 1024


def block_of(size, limit):
    tiles = size // 128
    best = 1
    for count in range(1, tiles + 1):
        if tiles % count == 0 and count * 128 <= limit:
            best = count
    return best * 128


def chunk_widths(width, shares):
    unit = 256 if width % 256 == 0 else 128
    tiles = width // unit
    ends = [round(tiles * sum(shares[: k + 1]) / sum(shares)) for k in range(len(shares))]
    counts = [end - start for start, end in zip([0] + ends, ends)]
    return [count * unit for count in counts if count > 0]


def over_count(values, count):
    if power_of_two(count):
        return values * (1.0 / count)
    return values / count


def standardize(values):
    count = values.shape[0]
    mean = over_count(jnp.sum(values, axis=0, keepdims=True), count)
    centred = values - mean
    var = over_count(jnp.sum(centred * centred, axis=0, keepdims=True), count)
    return (centred * lax.rsqrt(var + EPS)).astype(jnp.bfloat16)


def power_of_two(count):
    return count & (count - 1) == 0


def partner(place, step, size):
    if power_of_two(size):
        return place ^ step
    return (place + step) % size


def cut_kernel(n_fa, n_fb, a_ref, b_ref, *refs):
    outs, sems = refs[:-1], refs[-1]
    width_a = a_ref.shape[1] // n_fa
    width_b = b_ref.shape[1] // n_fb
    fa = lax.axis_index("fa")
    fb = lax.axis_index("fb")
    copies = []
    for step in range(n_fa):
        start = pl.multiple_of(partner(fa, step, n_fa) * width_a, 128)
        copies.append((a_ref.at[:, pl.ds(start, width_a)], outs[step]))
    for step in range(n_fb):
        start = pl.multiple_of(partner(fb, step, n_fb) * width_b, 128)
        copies.append((b_ref.at[:, pl.ds(start, width_b)], outs[n_fa + step]))
    started = []
    for place, (src, dst) in enumerate(copies):
        copy = pltpu.make_async_copy(src, dst, sems.at[place])
        copy.start()
        started.append(copy)
    for copy in started:
        copy.wait()


def cut_panels(a_acts, b_acts, n_fa, n_fb):
    tok, width = a_acts.shape
    shapes = [jax.ShapeDtypeStruct((tok, width // n_fa), a_acts.dtype)] * n_fa
    shapes += [jax.ShapeDtypeStruct((tok, width // n_fb), b_acts.dtype)] * n_fb
    outs = pl.pallas_call(
        functools.partial(cut_kernel, n_fa, n_fb),
        out_shape=shapes,
        in_specs=[pl.BlockSpec(memory_space=pltpu.HBM)] * 2,
        out_specs=[pl.BlockSpec(memory_space=pltpu.VMEM)] * len(shapes),
        scratch_shapes=[pltpu.SemaphoreType.DMA((len(shapes),))],
        compiler_params=pltpu.CompilerParams(vmem_limit_bytes=VMEM),
        name="cut_panels",
    )(a_acts, b_acts)
    return outs[:n_fa], outs[n_fa:]


def join_kernel(shapes, *refs):
    n_in = sum(len_in for len_in, _ in shapes)
    n_out = sum(len_out for _, len_out in shapes)
    ins, outs = refs[:n_in], refs[-n_out:]
    for len_in, len_out in shapes:
        tok = ins[0].shape[0]
        column = 0
        for out in outs[:len_out]:
            width = out.shape[1]
            for i in range(len_in):
                out[pl.ds(i * tok, tok), :] = ins[i][:, pl.ds(column, width)]
            column += width
        ins, outs = ins[len_in:], outs[len_out:]


def join_rows(groups, after=()):
    pieces = [piece for group, _ in groups for piece in group]
    shapes = [
        jax.ShapeDtypeStruct((group[0].shape[0] * len(group), width), group[0].dtype)
        for group, widths in groups
        for width in widths
    ]
    return pl.pallas_call(
        functools.partial(join_kernel, [(len(group), len(widths)) for group, widths in groups]),
        out_shape=shapes,
        in_specs=[pl.BlockSpec(memory_space=pltpu.VMEM)] * len(pieces)
        + [pl.BlockSpec(memory_space=pl.ANY)] * len(after),
        out_specs=[pl.BlockSpec(memory_space=pltpu.VMEM)] * len(shapes),
        compiler_params=pltpu.CompilerParams(vmem_limit_bytes=VMEM),
        name="join_rows",
    )(*pieces, *after)


def stacked(pieces, after=()):
    return join_rows([(pieces, [pieces[0].shape[1]])], after)[0]


def standardize_a_kernel(n_fa, n_fb, *refs):
    groups, out = refs[:n_fb], refs[-1]
    tok = groups[0].shape[0] // n_fa
    pieces = [
        group[pl.ds(i * tok, tok), :].astype(jnp.float32) for i in range(n_fa) for group in groups
    ]
    out[...] = standardize(jnp.concatenate(pieces, axis=0)).T


def standardize_a(groups, n_fa, n_fb):
    rows, width = groups[0].shape
    block = block_of(width, 512)
    total = rows * n_fb
    return pl.pallas_call(
        functools.partial(standardize_a_kernel, n_fa, n_fb),
        out_shape=jax.ShapeDtypeStruct((width, total), jnp.bfloat16),
        grid=(width // block,),
        in_specs=[pl.BlockSpec((rows, block), lambda i: (0, i))] * n_fb,
        out_specs=pl.BlockSpec((block, total), lambda i: (i, 0)),
        compiler_params=pltpu.CompilerParams(vmem_limit_bytes=VMEM),
        cost_estimate=pl.CostEstimate(
            flops=10 * width * total, bytes_accessed=4 * width * total, transcendentals=0
        ),
        name="standardize_a",
    )(*groups)


def product_kernel(n_groups, column, a_ref, *refs):
    groups = refs[:n_groups]
    out, slots, sems = refs[-3:]
    total, width = a_ref.shape[1], groups[0].shape[1]
    n_slots, height, strip = slots.shape

    def copy_of(step):
        slot = lax.rem(step, n_slots)
        place = pl.multiple_of(column + step * strip, 128)
        return pltpu.make_async_copy(slots.at[slot], out.at[:, pl.ds(place, strip)], sems.at[slot])

    @pl.loop(0, width // strip)
    def _(step):
        @pl.when(step >= n_slots)
        def _():
            copy_of(step - n_slots).wait()

        parts = []
        for part in range(strip // 128):
            columns = pl.ds(pl.multiple_of(step * strip + part * 128, 128), 128)
            pieces = [ref[:, columns].astype(jnp.float32) for ref in groups]
            parts.append(standardize(jnp.concatenate(pieces, axis=0)))
        std = jnp.concatenate(parts, axis=1)
        product = jnp.dot(a_ref[...], std, preferred_element_type=jnp.float32)
        slots[lax.rem(step, n_slots)] = over_count(product, total)
        copy_of(step).start()

    @pl.loop(max(width // strip - n_slots, 0), width // strip)
    def _(step):
        copy_of(step).wait()


def product_chunk(std_a, groups, column, full_width, buffer, after=()):
    height, total = std_a.shape
    width = groups[0].shape[1]
    strip = 256 if width % 256 == 0 else 128
    n_slots = 4
    in_specs = [pl.BlockSpec(memory_space=pltpu.VMEM)] * (1 + len(groups))
    in_specs += [pl.BlockSpec(memory_space=pl.ANY)] * len(after)
    args = [std_a, *groups, *after]
    aliases = {}
    if buffer is not None:
        aliases = {len(args): 0}
        in_specs.append(pl.BlockSpec(memory_space=pl.ANY))
        args.append(buffer)
    return pl.pallas_call(
        functools.partial(product_kernel, len(groups), column),
        out_shape=jax.ShapeDtypeStruct((height, full_width), jnp.float32),
        in_specs=in_specs,
        out_specs=pl.BlockSpec(memory_space=pl.ANY),
        scratch_shapes=[
            pltpu.VMEM((n_slots, height, strip), jnp.float32),
            pltpu.SemaphoreType.DMA((n_slots,)),
        ],
        input_output_aliases=aliases,
        compiler_params=pltpu.CompilerParams(vmem_limit_bytes=VMEM),
        cost_estimate=pl.CostEstimate(
            flops=2 * height * width * total, bytes_accessed=4 * height * width, transcendentals=0
        ),
        name="product_chunk",
    )(*args)


def sent(x, axis, step):
    size = lax.axis_size(axis)
    return lax.ppermute(x, axis, [(i, partner(i, step, size)) for i in range(size)])


def per_device(a_acts, b_acts):
    n_fa = lax.axis_size("fa")
    n_fb = lax.axis_size("fb")
    panels_a, panels_b = cut_panels(a_acts, b_acts, n_fa, n_fb)
    own_a = [panels_a[0]] + [sent(panels_a[s], "fa", s) for s in range(1, n_fa)]
    own_b = [panels_b[0]] + [sent(panels_b[s], "fb", s) for s in range(1, n_fb)]
    width_a, full_width = panels_a[0].shape[1], panels_b[0].shape[1]
    widths = chunk_widths(full_width, (1, 1))
    group_a, *parts_b = join_rows([(own_a, [width_a]), (own_b, widths), (own_b, [full_width])])
    group_b = parts_b.pop()

    whole = sent(group_b, "fa", 1)
    chunks = []
    for part in parts_b:
        blocks = [part, None]
        for step in range(2, n_fa):
            low = step & -step
            forward = power_of_two(n_fa) and low != step
            if forward and blocks[step - low] is not None:
                blocks.append(sent(blocks[step - low], "fa", low))
            else:
                blocks.append(sent(part, "fa", step))
        chunks.append(blocks)
    for blocks, block in zip(chunks, join_rows([([whole], widths)])):
        blocks[1] = block

    all_a = [group_a]
    for step in range(1, n_fb):
        low = step & -step
        if power_of_two(n_fb) and low != step:
            all_a.append(sent(stacked([all_a[step-low]],[chunks[0][2]]), "fb", low))
        else:
            all_a.append(sent(group_a, "fb", step))
    std_a = standardize_a(all_a, n_fa, n_fb)
    buffer = None
    column = 0
    for place, groups in enumerate(chunks):
        after = [later[2] for later in chunks[place + 1 : place + 2]]
        buffer = product_chunk(std_a, groups, column, full_width, buffer, after)
        column += groups[0].shape[1]
    return buffer


def solution(mesh):
    placed = (P(("layers", "fa", "fb"), None), P(("layers", "fa", "fb"), None))
    return jax.shard_map(
        per_device, mesh=mesh, in_specs=placed, out_specs=P(("layers", "fa"), "fb"), check_vma=False
    )
```

```python
import functools

import jax
import jax.numpy as jnp
from jax import lax
from jax.experimental import pallas as pl
from jax.experimental.pallas import tpu as pltpu
from jax.sharding import PartitionSpec as P

EPS = 1e-05
VMEM = 48 * 1024 * 1024


def block_of(size, limit):
    tiles = size // 128
    best = 1
    for count in range(1, tiles + 1):
        if tiles % count == 0 and count * 128 <= limit:
            best = count
    return best * 128


def chunk_widths(width, shares):
    unit = 256 if width % 256 == 0 else 128
    tiles = width // unit
    ends = [round(tiles * sum(shares[: k + 1]) / sum(shares)) for k in range(len(shares))]
    counts = [end - start for start, end in zip([0] + ends, ends)]
    return [count * unit for count in counts if count > 0]


def over_count(values, count):
    if power_of_two(count):
        return values * (1.0 / count)
    return values / count


def standardize(values):
    count = values.shape[0]
    mean = over_count(jnp.sum(values, axis=0, keepdims=True), count)
    centred = values - mean
    var = over_count(jnp.sum(centred * centred, axis=0, keepdims=True), count)
    return (centred * lax.rsqrt(var + EPS)).astype(jnp.bfloat16)


def power_of_two(count):
    return count & (count - 1) == 0


def partner(place, step, size):
    if power_of_two(size):
        return place ^ step
    return (place + step) % size


def cut_kernel(n_fa, n_fb, a_ref, b_ref, *refs):
    outs, sems = refs[:-1], refs[-1]
    width_a = a_ref.shape[1] // n_fa
    width_b = b_ref.shape[1] // n_fb
    fa = lax.axis_index("fa")
    fb = lax.axis_index("fb")
    copies = []
    for step in range(n_fa):
        start = pl.multiple_of(partner(fa, step, n_fa) * width_a, 128)
        copies.append((a_ref.at[:, pl.ds(start, width_a)], outs[step]))
    for step in range(n_fb):
        start = pl.multiple_of(partner(fb, step, n_fb) * width_b, 128)
        copies.append((b_ref.at[:, pl.ds(start, width_b)], outs[n_fa + step]))
    started = []
    for place, (src, dst) in enumerate(copies):
        copy = pltpu.make_async_copy(src, dst, sems.at[place])
        copy.start()
        started.append(copy)
    for copy in started:
        copy.wait()


def cut_panels(a_acts, b_acts, n_fa, n_fb):
    tok, width = a_acts.shape
    shapes = [jax.ShapeDtypeStruct((tok, width // n_fa), a_acts.dtype)] * n_fa
    shapes += [jax.ShapeDtypeStruct((tok, width // n_fb), b_acts.dtype)] * n_fb
    outs = pl.pallas_call(
        functools.partial(cut_kernel, n_fa, n_fb),
        out_shape=shapes,
        in_specs=[pl.BlockSpec(memory_space=pltpu.HBM)] * 2,
        out_specs=[pl.BlockSpec(memory_space=pltpu.VMEM)] * len(shapes),
        scratch_shapes=[pltpu.SemaphoreType.DMA((len(shapes),))],
        compiler_params=pltpu.CompilerParams(vmem_limit_bytes=VMEM),
        name="cut_panels",
    )(a_acts, b_acts)
    return outs[:n_fa], outs[n_fa:]


def join_kernel(shapes, *refs):
    n_in = sum(len_in for len_in, _, _ in shapes)
    n_out = sum(len_out for _, len_out, _ in shapes)
    ins, outs = refs[:n_in], refs[-n_out:]
    for len_in, len_out, column in shapes:
        tok = ins[0].shape[0]
        for out in outs[:len_out]:
            width = out.shape[1]
            for i in range(len_in):
                out[pl.ds(i * tok, tok), :] = ins[i][:, pl.ds(column, width)]
            column += width
        ins, outs = ins[len_in:], outs[len_out:]


def join_rows(groups, after=()):
    pieces = [piece for group, _, _ in groups for piece in group]
    shapes = [
        jax.ShapeDtypeStruct((group[0].shape[0] * len(group), width), group[0].dtype)
        for group, widths, _ in groups
        for width in widths
    ]
    return pl.pallas_call(
        functools.partial(join_kernel, [(len(group), len(widths), column) for group, widths, column in groups]),
        out_shape=shapes,
        in_specs=[pl.BlockSpec(memory_space=pltpu.VMEM)] * len(pieces)
        + [pl.BlockSpec(memory_space=pl.ANY)] * len(after),
        out_specs=[pl.BlockSpec(memory_space=pltpu.VMEM)] * len(shapes),
        compiler_params=pltpu.CompilerParams(vmem_limit_bytes=VMEM),
        name="join_rows",
    )(*pieces, *after)


def stacked(pieces, after=()):
    return join_rows([(pieces, [pieces[0].shape[1]], 0)], after)[0]


def standardize_a_kernel(n_fa, n_fb, *refs):
    groups, out = refs[:n_fb], refs[-1]
    tok = groups[0].shape[0] // n_fa
    pieces = [
        group[pl.ds(i * tok, tok), :].astype(jnp.float32) for i in range(n_fa) for group in groups
    ]
    out[...] = standardize(jnp.concatenate(pieces, axis=0)).T


def standardize_a(groups, n_fa, n_fb):
    rows, width = groups[0].shape
    block = block_of(width, 512)
    total = rows * n_fb
    return pl.pallas_call(
        functools.partial(standardize_a_kernel, n_fa, n_fb),
        out_shape=jax.ShapeDtypeStruct((width, total), jnp.bfloat16),
        grid=(width // block,),
        in_specs=[pl.BlockSpec((rows, block), lambda i: (0, i))] * n_fb,
        out_specs=pl.BlockSpec((block, total), lambda i: (i, 0)),
        compiler_params=pltpu.CompilerParams(vmem_limit_bytes=VMEM),
        cost_estimate=pl.CostEstimate(
            flops=10 * width * total, bytes_accessed=4 * width * total, transcendentals=0
        ),
        name="standardize_a",
    )(*groups)


def product_kernel(n_groups, column, a_ref, *refs):
    groups = refs[:n_groups]
    out, token, slots, sems = refs[-4:]
    token[...] = jnp.zeros_like(token)
    total, width = a_ref.shape[1], groups[0].shape[1]
    n_slots, height, strip = slots.shape

    def copy_of(step):
        slot = lax.rem(step, n_slots)
        place = pl.multiple_of(column + step * strip, 128)
        return pltpu.make_async_copy(slots.at[slot], out.at[:, pl.ds(place, strip)], sems.at[slot])

    @pl.loop(0, width // strip)
    def _(step):
        @pl.when(step >= n_slots)
        def _():
            copy_of(step - n_slots).wait()

        parts = []
        for part in range(strip // 128):
            columns = pl.ds(pl.multiple_of(step * strip + part * 128, 128), 128)
            pieces = [ref[:, columns].astype(jnp.float32) for ref in groups]
            parts.append(standardize(jnp.concatenate(pieces, axis=0)))
        std = jnp.concatenate(parts, axis=1)
        product = jnp.dot(a_ref[...], std, preferred_element_type=jnp.float32)
        slots[lax.rem(step, n_slots)] = over_count(product, total)
        copy_of(step).start()

    @pl.loop(max(width // strip - n_slots, 0), width // strip)
    def _(step):
        copy_of(step).wait()


def product_chunk(std_a, groups, column, full_width, buffer, after=()):
    height, total = std_a.shape
    width = groups[0].shape[1]
    strip = 256 if width % 256 == 0 else 128
    n_slots = 4
    in_specs = [pl.BlockSpec(memory_space=pltpu.VMEM)] * (1 + len(groups))
    in_specs += [pl.BlockSpec(memory_space=pl.ANY)] * len(after)
    args = [std_a, *groups, *after]
    aliases = {}
    if buffer is not None:
        aliases = {len(args): 0}
        in_specs.append(pl.BlockSpec(memory_space=pl.ANY))
        args.append(buffer)
    return pl.pallas_call(
        functools.partial(product_kernel, len(groups), column),
        out_shape=[
            jax.ShapeDtypeStruct((height, full_width), jnp.float32),
            jax.ShapeDtypeStruct((8, 128), jnp.float32),
        ],
        in_specs=in_specs,
        out_specs=[pl.BlockSpec(memory_space=pl.ANY), pl.BlockSpec(memory_space=pltpu.VMEM)],
        scratch_shapes=[
            pltpu.VMEM((n_slots, height, strip), jnp.float32),
            pltpu.SemaphoreType.DMA((n_slots,)),
        ],
        input_output_aliases=aliases,
        compiler_params=pltpu.CompilerParams(vmem_limit_bytes=VMEM),
        cost_estimate=pl.CostEstimate(
            flops=2 * height * width * total, bytes_accessed=4 * height * width, transcendentals=0
        ),
        name="product_chunk",
    )(*args)


def sent(x, axis, step):
    size = lax.axis_size(axis)
    return lax.ppermute(x, axis, [(i, partner(i, step, size)) for i in range(size)])


def forwarded(block, axis, step, blocks, after=()):
    low = step & -step
    if power_of_two(lax.axis_size(axis)):
        held = blocks[step - low]
        return sent(stacked([held], after) if after else held, axis, low)
    return sent(block, axis, step)


def per_device(a_acts, b_acts):
    n_fa = lax.axis_size("fa")
    n_fb = lax.axis_size("fb")
    panels_a, panels_b = cut_panels(a_acts, b_acts, n_fa, n_fb)
    own_a = [panels_a[0]] + [sent(panels_a[s], "fa", s) for s in range(1, n_fa)]
    own_b = [panels_b[0]] + [sent(panels_b[s], "fb", s) for s in range(1, n_fb)]
    width_a, full_width = panels_a[0].shape[1], panels_b[0].shape[1]
    widths = chunk_widths(full_width, (4, 5, 5))
    group_a, *parts_b, rest = join_rows(
        [(own_a, [width_a], 0), (own_b, widths, 0), (own_b, [sum(widths[1:])], widths[0])]
    )
    near = sent(parts_b[0], "fa", 1)

    chunks = []
    for place, part in enumerate(parts_b):
        if place:
            part = stacked([part], [chunks[-1][2]])
        chunks.append([part, near, sent(part, "fa", 2)])
    near_rest = sent(stacked([rest], [chunks[0][2]]), "fa", 1)

    all_a = [group_a]
    for step in range(1, n_fb):
        if power_of_two(step):
            all_a.append(sent(group_a, "fb", step))
        else:
            all_a.append(forwarded(group_a, "fb", step, all_a, chunks[0][1:3]))
    std_a = standardize_a(all_a, n_fa, n_fb)

    buffer = None
    column = 0
    done = []
    for place, groups in enumerate(chunks):
        hold = [[], [std_a], done[:1]][min(place, 2)]
        if place == 1:
            for later, block in zip(chunks[1:], join_rows([([near_rest], widths[1:], 0)], done)):
                later[1] = block
        for step in range(3, n_fa):
            if power_of_two(step):
                groups.append(sent(groups[0], "fa", step))
            else:
                groups.append(forwarded(groups[0], "fa", step, groups, hold if step == 3 else ()))
        after = [later[2] for later in chunks[place + 1 : place + 2]]
        buffer, token = product_chunk(std_a, groups, column, full_width, buffer, after)
        done.append(token)
        column += groups[0].shape[1]
    return buffer


def solution(mesh):
    placed = (P(("layers", "fa", "fb"), None), P(("layers", "fa", "fb"), None))
    return jax.shard_map(
        per_device, mesh=mesh, in_specs=placed, out_specs=P(("layers", "fa"), "fb"), check_vma=False
    )
```

```python
import functools

import jax
import jax.numpy as jnp
from jax import lax
from jax.experimental import pallas as pl
from jax.experimental.pallas import tpu as pltpu
from jax.sharding import PartitionSpec as P

EPS = 1e-05
VMEM = 48 * 1024 * 1024


def block_of(size, limit):
    tiles = size // 128
    best = 1
    for count in range(1, tiles + 1):
        if tiles % count == 0 and count * 128 <= limit:
            best = count
    return best * 128


def chunk_widths(width, shares):
    unit = 256 if width % 256 == 0 else 128
    tiles = width // unit
    ends = [round(tiles * sum(shares[: k + 1]) / sum(shares)) for k in range(len(shares))]
    counts = [end - start for start, end in zip([0] + ends, ends)]
    return [count * unit for count in counts if count > 0]


def over_count(values, count):
    if power_of_two(count):
        return values * (1.0 / count)
    return values / count


def standardize(values):
    count = values.shape[0]
    mean = over_count(jnp.sum(values, axis=0, keepdims=True), count)
    centred = values - mean
    var = over_count(jnp.sum(centred * centred, axis=0, keepdims=True), count)
    return (centred * lax.rsqrt(var + EPS)).astype(jnp.bfloat16)


def power_of_two(count):
    return count & (count - 1) == 0


def partner(place, step, size):
    if power_of_two(size):
        return place ^ step
    return (place + step) % size


def cut_kernel(n_fa, n_fb, a_ref, b_ref, *refs):
    outs, sems = refs[:-1], refs[-1]
    width_a = a_ref.shape[1] // n_fa
    width_b = b_ref.shape[1] // n_fb
    fa = lax.axis_index("fa")
    fb = lax.axis_index("fb")
    copies = []
    for step in range(n_fa):
        start = pl.multiple_of(partner(fa, step, n_fa) * width_a, 128)
        copies.append((a_ref.at[:, pl.ds(start, width_a)], outs[step]))
    for step in range(n_fb):
        start = pl.multiple_of(partner(fb, step, n_fb) * width_b, 128)
        copies.append((b_ref.at[:, pl.ds(start, width_b)], outs[n_fa + step]))
    started = []
    for place, (src, dst) in enumerate(copies):
        copy = pltpu.make_async_copy(src, dst, sems.at[place])
        copy.start()
        started.append(copy)
    for copy in started:
        copy.wait()


def cut_panels(a_acts, b_acts, n_fa, n_fb):
    tok, width = a_acts.shape
    shapes = [jax.ShapeDtypeStruct((tok, width // n_fa), a_acts.dtype)] * n_fa
    shapes += [jax.ShapeDtypeStruct((tok, width // n_fb), b_acts.dtype)] * n_fb
    outs = pl.pallas_call(
        functools.partial(cut_kernel, n_fa, n_fb),
        out_shape=shapes,
        in_specs=[pl.BlockSpec(memory_space=pltpu.HBM)] * 2,
        out_specs=[pl.BlockSpec(memory_space=pltpu.VMEM)] * len(shapes),
        scratch_shapes=[pltpu.SemaphoreType.DMA((len(shapes),))],
        compiler_params=pltpu.CompilerParams(vmem_limit_bytes=60*1024*1024),
        name="cut_panels",
    )(a_acts, b_acts)
    return outs[:n_fa], outs[n_fa:]


def join_kernel(shapes, *refs):
    n_in = sum(len_in for len_in, _, _ in shapes)
    n_out = sum(len_out for _, len_out, _ in shapes)
    ins, outs = refs[:n_in], refs[-n_out:]
    for len_in, len_out, column in shapes:
        tok = ins[0].shape[0]
        for out in outs[:len_out]:
            width = out.shape[1]
            for i in range(len_in):
                out[pl.ds(i * tok, tok), :] = ins[i][:, pl.ds(column, width)]
            column += width
        ins, outs = ins[len_in:], outs[len_out:]


def join_rows(groups, after=()):
    pieces = [piece for group, _, _ in groups for piece in group]
    shapes = [
        jax.ShapeDtypeStruct((group[0].shape[0] * len(group), width), group[0].dtype)
        for group, widths, _ in groups
        for width in widths
    ]
    return pl.pallas_call(
        functools.partial(join_kernel, [(len(group), len(widths), column) for group, widths, column in groups]),
        out_shape=shapes,
        in_specs=[pl.BlockSpec(memory_space=pltpu.VMEM)] * len(pieces)
        + [pl.BlockSpec(memory_space=pl.ANY)] * len(after),
        out_specs=[pl.BlockSpec(memory_space=pltpu.VMEM)] * len(shapes),
        compiler_params=pltpu.CompilerParams(vmem_limit_bytes=VMEM),
        name="join_rows",
    )(*pieces, *after)


def stacked(pieces, after=()):
    return join_rows([(pieces, [pieces[0].shape[1]], 0)], after)[0]


def standardize_a_kernel(n_fa, n_fb, *refs):
    groups, out = refs[:n_fb], refs[-1]
    tok = groups[0].shape[0] // n_fa
    pieces = [
        group[pl.ds(i * tok, tok), :].astype(jnp.float32) for i in range(n_fa) for group in groups
    ]
    out[...] = standardize(jnp.concatenate(pieces, axis=0)).T


def standardize_a(groups, n_fa, n_fb):
    rows, width = groups[0].shape
    block = block_of(width, 512)
    total = rows * n_fb
    return pl.pallas_call(
        functools.partial(standardize_a_kernel, n_fa, n_fb),
        out_shape=jax.ShapeDtypeStruct((width, total), jnp.bfloat16),
        grid=(width // block,),
        in_specs=[pl.BlockSpec((rows, block), lambda i: (0, i))] * n_fb,
        out_specs=pl.BlockSpec((block, total), lambda i: (i, 0)),
        compiler_params=pltpu.CompilerParams(vmem_limit_bytes=VMEM),
        cost_estimate=pl.CostEstimate(
            flops=10 * width * total, bytes_accessed=4 * width * total, transcendentals=0
        ),
        name="standardize_a",
    )(*groups)


def product_kernel(n_groups, column, a_ref, *refs):
    groups = refs[:n_groups]
    out, slots, sems = refs[-3:]
    total, width = a_ref.shape[1], groups[0].shape[1]
    n_slots, height, strip = slots.shape

    def copy_of(step):
        slot = lax.rem(step, n_slots)
        place = pl.multiple_of(column + step * strip, 128)
        return pltpu.make_async_copy(slots.at[slot], out.at[:, pl.ds(place, strip)], sems.at[slot])

    @pl.loop(0, width // strip)
    def _(step):
        @pl.when(step >= n_slots)
        def _():
            copy_of(step - n_slots).wait()

        parts = []
        for part in range(strip // 128):
            columns = pl.ds(pl.multiple_of(step * strip + part * 128, 128), 128)
            pieces = [ref[:, columns].astype(jnp.float32) for ref in groups]
            parts.append(standardize(jnp.concatenate(pieces, axis=0)))
        std = jnp.concatenate(parts, axis=1)
        product = jnp.dot(a_ref[...], std, preferred_element_type=jnp.float32)
        slots[lax.rem(step, n_slots)] = over_count(product, total)
        copy_of(step).start()

    @pl.loop(max(width // strip - n_slots, 0), width // strip)
    def _(step):
        copy_of(step).wait()


def product_chunk(std_a, groups, column, full_width, buffer, after=()):
    height, total = std_a.shape
    width = groups[0].shape[1]
    strip = 256 if width % 256 == 0 else 128
    n_slots = 4
    in_specs = [pl.BlockSpec(memory_space=pltpu.VMEM)] * (1 + len(groups))
    in_specs += [pl.BlockSpec(memory_space=pl.ANY)] * len(after)
    args = [std_a, *groups, *after]
    aliases = {}
    if buffer is not None:
        aliases = {len(args): 0}
        in_specs.append(pl.BlockSpec(memory_space=pl.ANY))
        args.append(buffer)
    return pl.pallas_call(
        functools.partial(product_kernel, len(groups), column),
        out_shape=jax.ShapeDtypeStruct((height, full_width), jnp.float32),
        in_specs=in_specs,
        out_specs=pl.BlockSpec(memory_space=pl.ANY),
        scratch_shapes=[
            pltpu.VMEM((n_slots, height, strip), jnp.float32),
            pltpu.SemaphoreType.DMA((n_slots,)),
        ],
        input_output_aliases=aliases,
        compiler_params=pltpu.CompilerParams(vmem_limit_bytes=VMEM),
        cost_estimate=pl.CostEstimate(
            flops=2 * height * width * total, bytes_accessed=4 * height * width, transcendentals=0
        ),
        name="product_chunk",
    )(*args)


def sent(x, axis, step):
    size = lax.axis_size(axis)
    return lax.ppermute(x, axis, [(i, partner(i, step, size)) for i in range(size)])


def forwarded(block, axis, step, blocks, after=()):
    low = step & -step
    if power_of_two(lax.axis_size(axis)):
        held = blocks[step - low]
        return sent(stacked([held], after) if after else held, axis, low)
    return sent(block, axis, step)


def per_device(a_acts, b_acts):
    n_fa = lax.axis_size("fa")
    n_fb = lax.axis_size("fb")
    panels_a, panels_b = cut_panels(a_acts, b_acts, n_fa, n_fb)
    own_a = [panels_a[0]] + [sent(panels_a[s], "fa", s) for s in range(1, n_fa)]
    own_b = [panels_b[0]] + [sent(panels_b[s], "fb", s) for s in range(1, n_fb)]
    width_a, full_width = panels_a[0].shape[1], panels_b[0].shape[1]
    widths = chunk_widths(full_width, (8, 6))
    group_a, *parts_b = join_rows([(own_a, [width_a], 0), (own_b, widths, 0)])

    first = parts_b[0]
    chunks = [[first, sent(first, "fa", 1), sent(first, "fa", 2)]]
    all_a = [group_a]
    for step in range(1, n_fb):
        if power_of_two(step):
            all_a.append(sent(group_a, "fb", step))
        else:
            all_a.append(forwarded(group_a, "fb", step, all_a, chunks[0][1:3]))
    std_a = standardize_a(all_a, n_fa, n_fb)
    for part in parts_b[1:]:
        part = stacked([part], chunks[-1][2:3])
        across = sent(part, "fa", 2)
        near = sent(stacked([part], [across, std_a]), "fa", 1)
        chunks.append([part, near, across])

    buffer = None
    column = 0
    for place, groups in enumerate(chunks):
        hold = [std_a] if place else []
        for step in range(3, n_fa):
            if power_of_two(step):
                groups.append(sent(groups[0], "fa", step))
            else:
                groups.append(forwarded(groups[0], "fa", step, groups, hold if step == 3 else ()))
        after = [later[2] for later in chunks[place + 1 : place + 2]]
        buffer = product_chunk(std_a, groups, column, full_width, buffer, after)
        column += groups[0].shape[1]
    return buffer


def solution(mesh):
    placed = (P(("layers", "fa", "fb"), None), P(("layers", "fa", "fb"), None))
    return jax.shard_map(
        per_device, mesh=mesh, in_specs=placed, out_specs=P(("layers", "fa"), "fb"), check_vma=False
    )
```

```python
import functools

import jax
import jax.numpy as jnp
from jax import lax
from jax.experimental import pallas as pl
from jax.experimental.pallas import tpu as pltpu
from jax.sharding import PartitionSpec as P

EPS = 1e-05
VMEM = 48 * 1024 * 1024


def block_of(size, limit):
    tiles = size // 128
    best = 1
    for count in range(1, tiles + 1):
        if tiles % count == 0 and count * 128 <= limit:
            best = count
    return best * 128


def chunk_widths(width, shares):
    unit = 256 if width % 256 == 0 else 128
    tiles = width // unit
    ends = [round(tiles * sum(shares[: k + 1]) / sum(shares)) for k in range(len(shares))]
    counts = [end - start for start, end in zip([0] + ends, ends)]
    return [count * unit for count in counts if count > 0]


def over_count(values, count):
    if power_of_two(count):
        return values * (1.0 / count)
    return values / count


def standardize(values):
    count = values.shape[0]
    mean = over_count(jnp.sum(values, axis=0, keepdims=True), count)
    centred = values - mean
    var = over_count(jnp.sum(centred * centred, axis=0, keepdims=True), count)
    return (centred * lax.rsqrt(var + EPS)).astype(jnp.bfloat16)


def power_of_two(count):
    return count & (count - 1) == 0


def partner(place, step, size):
    if power_of_two(size):
        return place ^ step
    return (place + step) % size


def cut_kernel(n_fa, n_fb, a_ref, b_ref, *refs):
    outs, sems = refs[:-1], refs[-1]
    width_a = a_ref.shape[1] // n_fa
    width_b = b_ref.shape[1] // n_fb
    fa = lax.axis_index("fa")
    fb = lax.axis_index("fb")
    copies = []
    for step in range(n_fa):
        start = pl.multiple_of(partner(fa, step, n_fa) * width_a, 128)
        copies.append((a_ref.at[:, pl.ds(start, width_a)], outs[step]))
    for step in range(n_fb):
        start = pl.multiple_of(partner(fb, step, n_fb) * width_b, 128)
        copies.append((b_ref.at[:, pl.ds(start, width_b)], outs[n_fa + step]))
    started = []
    for place, (src, dst) in enumerate(copies):
        copy = pltpu.make_async_copy(src, dst, sems.at[place])
        copy.start()
        started.append(copy)
    for copy in started:
        copy.wait()


def cut_panels(a_acts, b_acts, n_fa, n_fb):
    tok, width = a_acts.shape
    shapes = [jax.ShapeDtypeStruct((tok, width // n_fa), a_acts.dtype)] * n_fa
    shapes += [jax.ShapeDtypeStruct((tok, width // n_fb), b_acts.dtype)] * n_fb
    outs = pl.pallas_call(
        functools.partial(cut_kernel, n_fa, n_fb),
        out_shape=shapes,
        in_specs=[pl.BlockSpec(memory_space=pltpu.HBM)] * 2,
        out_specs=[pl.BlockSpec(memory_space=pltpu.VMEM)] * len(shapes),
        scratch_shapes=[pltpu.SemaphoreType.DMA((len(shapes),))],
        compiler_params=pltpu.CompilerParams(vmem_limit_bytes=VMEM),
        name="cut_panels",
    )(a_acts, b_acts)
    return outs[:n_fa], outs[n_fa:]


def join_kernel(shapes, *refs):
    n_in = sum(len_in for len_in, _, _ in shapes)
    n_out = sum(len_out for _, len_out, _ in shapes)
    ins, outs = refs[:n_in], refs[-n_out:]
    for len_in, len_out, column in shapes:
        tok = ins[0].shape[0]
        for out in outs[:len_out]:
            width = out.shape[1]
            for i in range(len_in):
                out[pl.ds(i * tok, tok), :] = ins[i][:, pl.ds(column, width)]
            column += width
        ins, outs = ins[len_in:], outs[len_out:]


def join_rows(groups, after=()):
    pieces = [piece for group, _, _ in groups for piece in group]
    shapes = [
        jax.ShapeDtypeStruct((group[0].shape[0] * len(group), width), group[0].dtype)
        for group, widths, _ in groups
        for width in widths
    ]
    return pl.pallas_call(
        functools.partial(join_kernel, [(len(group), len(widths), column) for group, widths, column in groups]),
        out_shape=shapes,
        in_specs=[pl.BlockSpec(memory_space=pltpu.VMEM)] * len(pieces)
        + [pl.BlockSpec(memory_space=pl.ANY)] * len(after),
        out_specs=[pl.BlockSpec(memory_space=pltpu.VMEM)] * len(shapes),
        compiler_params=pltpu.CompilerParams(vmem_limit_bytes=VMEM),
        name="join_rows",
    )(*pieces, *after)


def stacked(pieces, after=()):
    return join_rows([(pieces, [pieces[0].shape[1]], 0)], after)[0]


def standardize_a_kernel(n_fa, n_fb, *refs):
    groups, out = refs[:n_fb], refs[-1]
    tok = groups[0].shape[0] // n_fa
    pieces = [
        group[pl.ds(i * tok, tok), :].astype(jnp.float32) for i in range(n_fa) for group in groups
    ]
    out[...] = standardize(jnp.concatenate(pieces, axis=0)).T


def standardize_a(groups, n_fa, n_fb):
    rows, width = groups[0].shape
    block = block_of(width, 512)
    total = rows * n_fb
    return pl.pallas_call(
        functools.partial(standardize_a_kernel, n_fa, n_fb),
        out_shape=jax.ShapeDtypeStruct((width, total), jnp.bfloat16),
        grid=(width // block,),
        in_specs=[pl.BlockSpec((rows, block), lambda i: (0, i))] * n_fb,
        out_specs=pl.BlockSpec((block, total), lambda i: (i, 0)),
        compiler_params=pltpu.CompilerParams(vmem_limit_bytes=VMEM),
        cost_estimate=pl.CostEstimate(
            flops=10 * width * total, bytes_accessed=4 * width * total, transcendentals=0
        ),
        name="standardize_a",
    )(*groups)


def product_kernel(n_groups, column, a_ref, *refs):
    groups = refs[:n_groups]
    out, slots, sems = refs[-3:]
    total, width = a_ref.shape[1], groups[0].shape[1]
    n_slots, height, strip = slots.shape

    def copy_of(step):
        slot = lax.rem(step, n_slots)
        place = pl.multiple_of(column + step * strip, 128)
        return pltpu.make_async_copy(slots.at[slot], out.at[:, pl.ds(place, strip)], sems.at[slot])

    @pl.loop(0, width // strip)
    def _(step):
        @pl.when(step >= n_slots)
        def _():
            copy_of(step - n_slots).wait()

        parts = []
        for part in range(strip // 128):
            columns = pl.ds(pl.multiple_of(step * strip + part * 128, 128), 128)
            pieces = [ref[:, columns].astype(jnp.float32) for ref in groups]
            parts.append(standardize(jnp.concatenate(pieces, axis=0)))
        std = jnp.concatenate(parts, axis=1)
        product = jnp.dot(a_ref[...], std, preferred_element_type=jnp.float32)
        slots[lax.rem(step, n_slots)] = over_count(product, total)
        copy_of(step).start()

    @pl.loop(max(width // strip - n_slots, 0), width // strip)
    def _(step):
        copy_of(step).wait()


def product_chunk(std_a, groups, column, full_width, buffer, after=()):
    height, total = std_a.shape
    width = groups[0].shape[1]
    strip = 256 if width % 256 == 0 else 128
    n_slots = 4
    in_specs = [pl.BlockSpec(memory_space=pltpu.VMEM)] * (1 + len(groups))
    in_specs += [pl.BlockSpec(memory_space=pl.ANY)] * len(after)
    args = [std_a, *groups, *after]
    aliases = {}
    if buffer is not None:
        aliases = {len(args): 0}
        in_specs.append(pl.BlockSpec(memory_space=pl.ANY))
        args.append(buffer)
    return pl.pallas_call(
        functools.partial(product_kernel, len(groups), column),
        out_shape=jax.ShapeDtypeStruct((height, full_width), jnp.float32),
        in_specs=in_specs,
        out_specs=pl.BlockSpec(memory_space=pl.ANY),
        scratch_shapes=[
            pltpu.VMEM((n_slots, height, strip), jnp.float32),
            pltpu.SemaphoreType.DMA((n_slots,)),
        ],
        input_output_aliases=aliases,
        compiler_params=pltpu.CompilerParams(vmem_limit_bytes=VMEM),
        cost_estimate=pl.CostEstimate(
            flops=2 * height * width * total, bytes_accessed=4 * height * width, transcendentals=0
        ),
        name="product_chunk",
    )(*args)


def sent(x, axis, step):
    size = lax.axis_size(axis)
    return lax.ppermute(x, axis, [(i, partner(i, step, size)) for i in range(size)])


def forwarded(block, axis, step, blocks, after=()):
    low = step & -step
    if power_of_two(lax.axis_size(axis)):
        held = blocks[step - low]
        return sent(stacked([held], after) if after else held, axis, low)
    return sent(block, axis, step)


def per_device(a_acts, b_acts):
    n_fa = lax.axis_size("fa")
    n_fb = lax.axis_size("fb")
    panels_a, panels_b = cut_panels(a_acts, b_acts, n_fa, n_fb)
    own_a = [panels_a[0]] + [sent(panels_a[s], "fa", s) for s in reversed(range(1, n_fa))]
    own_b = [panels_b[0]] + [sent(panels_b[s], "fb", s) for s in range(1, n_fb)]
    width_a, full_width = panels_a[0].shape[1], panels_b[0].shape[1]
    widths = chunk_widths(full_width, (8, 6))
    group_a, *parts_b = join_rows([(own_a, [width_a], 0), (own_b, widths, 0)])

    def forward(groups, hold):
        for step in range(3, n_fa):
            if power_of_two(step):
                groups.append(sent(groups[0], "fa", step))
            else:
                groups.append(forwarded(groups[0], "fa", step, groups, hold if step == 3 else ()))

    first = parts_b[0]
    chunks = [[first, sent(first, "fa", 1), sent(first, "fa", 2)]]
    forward(chunks[0], ())
    all_a = [group_a]
    for step in range(1, n_fb):
        if power_of_two(step):
            all_a.append(sent(group_a, "fb", step))
        else:
            all_a.append(forwarded(group_a, "fb", step, all_a, chunks[0][1:3]))
    std_a = standardize_a(all_a, n_fa, n_fb)
    for part in parts_b[1:]:
        across = sent(stacked([part], chunks[-1][2:3]), "fa", 2)
        near = sent(stacked([part], [chunks[-1][3], std_a]), "fa", 1)
        groups = [part, near, across]
        forward(groups, [std_a])
        chunks.append(groups)

    buffer = None
    column = 0
    for place, groups in enumerate(chunks):
        after = [later[2] for later in chunks[place + 1 : place + 2]]
        ordered = groups[:1] + groups[:0:-1]
        buffer = product_chunk(std_a, ordered, column, full_width, buffer, after)
        column += groups[0].shape[1]
    return buffer


def solution(mesh):
    placed = (P(("layers", "fa", "fb"), None), P(("layers", "fa", "fb"), None))
    return jax.shard_map(
        per_device, mesh=mesh, in_specs=placed, out_specs=P(("layers", "fa"), "fb"), check_vma=False
    )
```

```python
import functools

import jax
import jax.numpy as jnp
from jax import lax
from jax.experimental import pallas as pl
from jax.experimental.pallas import tpu as pltpu
from jax.sharding import PartitionSpec as P

EPS = 1e-05
VMEM = 48 * 1024 * 1024


def block_of(size, limit):
    tiles = size // 128
    best = 1
    for count in range(1, tiles + 1):
        if tiles % count == 0 and count * 128 <= limit:
            best = count
    return best * 128


def chunk_widths(width, shares):
    unit = 256 if width % 256 == 0 else 128
    tiles = width // unit
    ends = [round(tiles * sum(shares[: k + 1]) / sum(shares)) for k in range(len(shares))]
    counts = [end - start for start, end in zip([0] + ends, ends)]
    return [count * unit for count in counts if count > 0]


def over_count(values, count):
    if power_of_two(count):
        return values * (1.0 / count)
    return values / count


def standardize(values):
    count = values.shape[0]
    mean = over_count(jnp.sum(values, axis=0, keepdims=True), count)
    centred = values - mean
    var = over_count(jnp.sum(centred * centred, axis=0, keepdims=True), count)
    return (centred * lax.rsqrt(var + EPS)).astype(jnp.bfloat16)


def power_of_two(count):
    return count & (count - 1) == 0


def partner(place, step, size):
    if power_of_two(size):
        return place ^ step
    return (place + step) % size


def cut_kernel(n_fa, n_fb, a_ref, b_ref, *refs):
    outs, sems = refs[:-1], refs[-1]
    width_a = a_ref.shape[1] // n_fa
    width_b = b_ref.shape[1] // n_fb
    fa = lax.axis_index("fa")
    fb = lax.axis_index("fb")
    copies = []
    for step in range(n_fa):
        start = pl.multiple_of(partner(fa, step, n_fa) * width_a, 128)
        copies.append((a_ref.at[:, pl.ds(start, width_a)], outs[step]))
    for step in range(n_fb):
        start = pl.multiple_of(partner(fb, step, n_fb) * width_b, 128)
        copies.append((b_ref.at[:, pl.ds(start, width_b)], outs[n_fa + step]))
    started = []
    for place, (src, dst) in enumerate(copies):
        copy = pltpu.make_async_copy(src, dst, sems.at[place])
        copy.start()
        started.append(copy)
    for copy in started:
        copy.wait()


def cut_panels(a_acts, b_acts, n_fa, n_fb):
    tok, width = a_acts.shape
    shapes = [jax.ShapeDtypeStruct((tok, width // n_fa), a_acts.dtype)] * n_fa
    shapes += [jax.ShapeDtypeStruct((tok, width // n_fb), b_acts.dtype)] * n_fb
    outs = pl.pallas_call(
        functools.partial(cut_kernel, n_fa, n_fb),
        out_shape=shapes,
        in_specs=[pl.BlockSpec(memory_space=pltpu.HBM)] * 2,
        out_specs=[pl.BlockSpec(memory_space=pltpu.VMEM)] * len(shapes),
        scratch_shapes=[pltpu.SemaphoreType.DMA((len(shapes),))],
        compiler_params=pltpu.CompilerParams(vmem_limit_bytes=VMEM),
        name="cut_panels",
    )(a_acts, b_acts)
    return outs[:n_fa], outs[n_fa:]


def join_kernel(shapes, *refs):
    n_in = sum(len_in for len_in, _, _ in shapes)
    n_out = sum(len_out for _, len_out, _ in shapes)
    ins, outs = refs[:n_in], refs[-n_out:]
    for len_in, len_out, column in shapes:
        tok = ins[0].shape[0]
        for out in outs[:len_out]:
            width = out.shape[1]
            for i in range(len_in):
                out[pl.ds(i * tok, tok), :] = ins[i][:, pl.ds(column, width)]
            column += width
        ins, outs = ins[len_in:], outs[len_out:]


def join_rows(groups, after=(), first=None):
    pieces = [piece for group, _, _ in groups for piece in group]
    order = list(range(len(pieces)))
    if first is not None:
        order.insert(0, order.pop(first))
    shapes = [
        jax.ShapeDtypeStruct((group[0].shape[0] * len(group), width), group[0].dtype)
        for group, widths, _ in groups
        for width in widths
    ]
    counts = [(len(group), len(widths), column) for group, widths, column in groups]

    def kernel(*refs):
        ins = [refs[order.index(place)] for place in range(len(pieces))]
        join_kernel(counts, *ins, *refs[len(pieces) :])

    return pl.pallas_call(
        kernel,
        out_shape=shapes,
        in_specs=[pl.BlockSpec(memory_space=pltpu.VMEM)] * len(pieces)
        + [pl.BlockSpec(memory_space=pl.ANY)] * len(after),
        out_specs=[pl.BlockSpec(memory_space=pltpu.VMEM)] * len(shapes),
        compiler_params=pltpu.CompilerParams(vmem_limit_bytes=VMEM),
        name="join_rows",
    )(*[pieces[place] for place in order], *after)


def stacked(pieces, after=()):
    return join_rows([(pieces, [pieces[0].shape[1]], 0)], after)[0]


def standardize_a_kernel(n_fa, n_fb, *refs):
    groups, out = refs[:n_fb], refs[-1]
    tok = groups[0].shape[0] // n_fa
    pieces = [
        group[pl.ds(i * tok, tok), :].astype(jnp.float32) for i in range(n_fa) for group in groups
    ]
    out[...] = standardize(jnp.concatenate(pieces, axis=0)).T


def standardize_a(groups, n_fa, n_fb):
    rows, width = groups[0].shape
    block = block_of(width, 512)
    total = rows * n_fb
    return pl.pallas_call(
        functools.partial(standardize_a_kernel, n_fa, n_fb),
        out_shape=jax.ShapeDtypeStruct((width, total), jnp.bfloat16),
        grid=(width // block,),
        in_specs=[pl.BlockSpec((rows, block), lambda i: (0, i))] * n_fb,
        out_specs=pl.BlockSpec((block, total), lambda i: (i, 0)),
        compiler_params=pltpu.CompilerParams(vmem_limit_bytes=VMEM),
        cost_estimate=pl.CostEstimate(
            flops=10 * width * total, bytes_accessed=4 * width * total, transcendentals=0
        ),
        name="standardize_a",
    )(*groups)


def product_kernel(n_groups, column, a_ref, *refs):
    groups = refs[:n_groups]
    out, slots, sems = refs[-3:]
    total, width = a_ref.shape[1], groups[0].shape[1]
    n_slots, height, strip = slots.shape

    def copy_of(step):
        slot = lax.rem(step, n_slots)
        place = pl.multiple_of(column + step * strip, 128)
        return pltpu.make_async_copy(slots.at[slot], out.at[:, pl.ds(place, strip)], sems.at[slot])

    @pl.loop(0, width // strip)
    def _(step):
        @pl.when(step >= n_slots)
        def _():
            copy_of(step - n_slots).wait()

        parts = []
        for part in range(strip // 128):
            columns = pl.ds(pl.multiple_of(step * strip + part * 128, 128), 128)
            pieces = [ref[:, columns].astype(jnp.float32) for ref in groups]
            parts.append(standardize(jnp.concatenate(pieces, axis=0)))
        std = jnp.concatenate(parts, axis=1)
        product = jnp.dot(a_ref[...], std, preferred_element_type=jnp.float32)
        slots[lax.rem(step, n_slots)] = over_count(product, total)
        copy_of(step).start()

    @pl.loop(max(width // strip - n_slots, 0), width // strip)
    def _(step):
        copy_of(step).wait()


def product_chunk(std_a, groups, column, full_width, buffer, after=()):
    height, total = std_a.shape
    width = groups[0].shape[1]
    strip = 256 if width % 256 == 0 else 128
    n_slots = 4
    in_specs = [pl.BlockSpec(memory_space=pltpu.VMEM)] * (1 + len(groups))
    in_specs += [pl.BlockSpec(memory_space=pl.ANY)] * len(after)
    args = [std_a, *groups, *after]
    aliases = {}
    if buffer is not None:
        aliases = {len(args): 0}
        in_specs.append(pl.BlockSpec(memory_space=pl.ANY))
        args.append(buffer)
    return pl.pallas_call(
        functools.partial(product_kernel, len(groups), column),
        out_shape=jax.ShapeDtypeStruct((height, full_width), jnp.float32),
        in_specs=in_specs,
        out_specs=pl.BlockSpec(memory_space=pl.ANY),
        scratch_shapes=[
            pltpu.VMEM((n_slots, height, strip), jnp.float32),
            pltpu.SemaphoreType.DMA((n_slots,)),
        ],
        input_output_aliases=aliases,
        compiler_params=pltpu.CompilerParams(vmem_limit_bytes=VMEM),
        cost_estimate=pl.CostEstimate(
            flops=2 * height * width * total, bytes_accessed=4 * height * width, transcendentals=0
        ),
        name="product_chunk",
    )(*args)


def sent(x, axis, step):
    size = lax.axis_size(axis)
    return lax.ppermute(x, axis, [(i, partner(i, step, size)) for i in range(size)])


def forwarded(block, axis, step, blocks, after=()):
    low = step & -step
    if power_of_two(lax.axis_size(axis)):
        held = blocks[step - low]
        return sent(stacked([held], after) if after else held, axis, low)
    return sent(block, axis, step)


def per_device(a_acts, b_acts):
    n_fa = lax.axis_size("fa")
    n_fb = lax.axis_size("fb")
    panels_a, panels_b = cut_panels(a_acts, b_acts, n_fa, n_fb)
    own_a = [panels_a[0]] + [sent(panels_a[s], "fa", s) for s in reversed(range(1, n_fa))]
    own_b = [panels_b[0]] + [sent(panels_b[s], "fb", s) for s in range(1, n_fb)]
    width_a, full_width = panels_a[0].shape[1], panels_b[0].shape[1]
    widths = chunk_widths(full_width, (1, 1))
    stacks = [(own_a, [width_a], 0), (own_b, widths, 0), (own_b, [full_width], 0)]
    group_a, *parts_b, group_b = join_rows(stacks, first=n_fa + 1)

    def forward(groups, hold):
        for step in range(3, n_fa):
            if power_of_two(step):
                groups.append(sent(groups[0], "fa", step))
            else:
                groups.append(forwarded(groups[0], "fa", step, groups, hold if step == 3 else ()))

    first = parts_b[0]
    whole = sent(group_b, "fa", 1)
    chunks = [[first, None, sent(first, "fa", 2)]]
    all_a = [group_a]
    for step in range(1, n_fb):
        if power_of_two(step):
            all_a.append(sent(group_a, "fb", step))
        else:
            all_a.append(forwarded(group_a, "fb", step, all_a, chunks[0][2:3]))
    std_a = standardize_a(all_a, n_fa, n_fb)
    for part in parts_b[1:]:
        across = sent(stacked([part], chunks[-1][2:3]), "fa", 2)
        chunks.append([part, None, across])
    for groups, near in zip(chunks, join_rows([([whole], widths, 0)])):
        groups[1] = near
    forward(chunks[0], ())
    for groups in chunks[1:]:
        forward(groups, [std_a])

    buffer = None
    column = 0
    for place, groups in enumerate(chunks):
        after = [later[2] for later in chunks[place + 1 : place + 2]]
        ordered = groups[:1] + groups[:0:-1]
        buffer = product_chunk(std_a, ordered, column, full_width, buffer, after)
        column += groups[0].shape[1]
    return buffer


def solution(mesh):
    placed = (P(("layers", "fa", "fb"), None), P(("layers", "fa", "fb"), None))
    return jax.shard_map(
        per_device, mesh=mesh, in_specs=placed, out_specs=P(("layers", "fa"), "fb"), check_vma=False
    )
```

```python
import functools

import jax
import jax.numpy as jnp
from jax import lax
from jax.experimental import pallas as pl
from jax.experimental.pallas import tpu as pltpu
from jax.sharding import PartitionSpec as P

EPS = 1e-05
VMEM = 48 * 1024 * 1024


def block_of(size, limit):
    tiles = size // 128
    best = 1
    for count in range(1, tiles + 1):
        if tiles % count == 0 and count * 128 <= limit:
            best = count
    return best * 128


def chunk_widths(width, shares):
    unit = 256 if width % 256 == 0 else 128
    tiles = width // unit
    ends = [round(tiles * sum(shares[: k + 1]) / sum(shares)) for k in range(len(shares))]
    counts = [end - start for start, end in zip([0] + ends, ends)]
    return [count * unit for count in counts if count > 0]


def over_count(values, count):
    if power_of_two(count):
        return values * (1.0 / count)
    return values / count


def standardize(values):
    count = values.shape[0]
    mean = over_count(jnp.sum(values, axis=0, keepdims=True), count)
    centred = values - mean
    var = over_count(jnp.sum(centred * centred, axis=0, keepdims=True), count)
    return (centred * lax.rsqrt(var + EPS)).astype(jnp.bfloat16)


def power_of_two(count):
    return count & (count - 1) == 0


def partner(place, step, size):
    if power_of_two(size):
        return place ^ step
    return (place + step) % size


def cut_kernel(axis, size, ref, *refs):
    outs, sems = refs[:-1], refs[-1]
    width = ref.shape[1] // size
    place = lax.axis_index(axis)
    started = []
    for step in range(size):
        start = pl.multiple_of(partner(place, step, size) * width, 128)
        copy = pltpu.make_async_copy(ref.at[:, pl.ds(start, width)], outs[step], sems.at[step])
        copy.start()
        started.append(copy)
    for copy in started:
        copy.wait()


def cut_panels(acts, axis):
    size = lax.axis_size(axis)
    tok, width = acts.shape
    return pl.pallas_call(
        functools.partial(cut_kernel, axis, size),
        out_shape=[jax.ShapeDtypeStruct((tok, width // size), acts.dtype)] * size,
        in_specs=[pl.BlockSpec(memory_space=pl.ANY)],
        out_specs=[pl.BlockSpec(memory_space=pltpu.VMEM)] * size,
        scratch_shapes=[pltpu.SemaphoreType.DMA((size,))],
        compiler_params=pltpu.CompilerParams(vmem_limit_bytes=VMEM),
        name="cut_panels",
    )(acts)


def join_kernel(shapes, *refs):
    n_in = sum(len_in for len_in, _, _ in shapes)
    n_out = sum(len_out for _, len_out, _ in shapes)
    ins, outs = refs[:n_in], refs[-n_out:]
    for len_in, len_out, column in shapes:
        tok = ins[0].shape[0]
        for out in outs[:len_out]:
            width = out.shape[1]
            for i in range(len_in):
                out[pl.ds(i * tok, tok), :] = ins[i][:, pl.ds(column, width)]
            column += width
        ins, outs = ins[len_in:], outs[len_out:]


def join_rows(groups, after=(), first=None):
    pieces = [piece for group, _, _ in groups for piece in group]
    order = list(range(len(pieces)))
    if first is not None:
        order.insert(0, order.pop(first))
    shapes = [
        jax.ShapeDtypeStruct((group[0].shape[0] * len(group), width), group[0].dtype)
        for group, widths, _ in groups
        for width in widths
    ]
    counts = [(len(group), len(widths), column) for group, widths, column in groups]

    def kernel(*refs):
        ins = [refs[order.index(place)] for place in range(len(pieces))]
        join_kernel(counts, *ins, *refs[len(pieces) :])

    return pl.pallas_call(
        kernel,
        out_shape=shapes,
        in_specs=[pl.BlockSpec(memory_space=pltpu.VMEM)] * len(pieces)
        + [pl.BlockSpec(memory_space=pl.ANY)] * len(after),
        out_specs=[pl.BlockSpec(memory_space=pltpu.VMEM)] * len(shapes),
        compiler_params=pltpu.CompilerParams(vmem_limit_bytes=VMEM),
        name="join_rows",
    )(*[pieces[place] for place in order], *after)


def stacked(pieces, after=()):
    return join_rows([(pieces, [pieces[0].shape[1]], 0)], after)[0]


def standardize_a_kernel(n_fa, n_fb, *refs):
    groups, out = refs[:n_fb], refs[-1]
    tok = groups[0].shape[0] // n_fa
    pieces = [
        group[pl.ds(i * tok, tok), :].astype(jnp.float32) for i in range(n_fa) for group in groups
    ]
    out[...] = standardize(jnp.concatenate(pieces, axis=0)).T


def standardize_a(groups, n_fa, n_fb):
    rows, width = groups[0].shape
    block = block_of(width, 512)
    total = rows * n_fb
    return pl.pallas_call(
        functools.partial(standardize_a_kernel, n_fa, n_fb),
        out_shape=jax.ShapeDtypeStruct((width, total), jnp.bfloat16),
        grid=(width // block,),
        in_specs=[pl.BlockSpec((rows, block), lambda i: (0, i))] * n_fb,
        out_specs=pl.BlockSpec((block, total), lambda i: (i, 0)),
        compiler_params=pltpu.CompilerParams(vmem_limit_bytes=VMEM),
        cost_estimate=pl.CostEstimate(
            flops=10 * width * total, bytes_accessed=4 * width * total, transcendentals=0
        ),
        name="standardize_a",
    )(*groups)


def product_kernel(n_groups, column, a_ref, *refs):
    groups = refs[:n_groups]
    out, slots, sems = refs[-3:]
    total, width = a_ref.shape[1], groups[0].shape[1]
    n_slots, height, strip = slots.shape
    n_parts = sems.shape[1]
    block = height // n_parts

    def copies_of(step, part):
        slot = lax.rem(step, n_slots)
        place = pl.multiple_of(column + step * strip, 128)
        rows = pl.ds(part * block, block)
        return pltpu.make_async_copy(
            slots.at[slot, rows], out.at[rows, pl.ds(place, strip)], sems.at[slot, part]
        )

    @pl.loop(0, width // strip)
    def _(step):
        parts = []
        for part in range(strip // 128):
            columns = pl.ds(pl.multiple_of(step * strip + part * 128, 128), 128)
            pieces = [ref[:, columns].astype(jnp.float32) for ref in groups]
            parts.append(standardize(jnp.concatenate(pieces, axis=0)))
        std = jnp.concatenate(parts, axis=1)
        for part in range(n_parts):
            rows = pl.ds(part * block, block)

            @pl.when(step >= n_slots)
            def _():
                copies_of(step - n_slots, part).wait()

            product = jnp.dot(a_ref[rows, :], std, preferred_element_type=jnp.float32)
            slots[lax.rem(step, n_slots), rows] = over_count(product, total)
            copies_of(step, part).start()

    @pl.loop(max(width // strip - n_slots, 0), width // strip)
    def _(step):
        for part in range(n_parts):
            copies_of(step, part).wait()


def product_chunk(std_a, groups, column, full_width, buffer, after=()):
    height, total = std_a.shape
    width = groups[0].shape[1]
    strip = 256 if width % 256 == 0 else 128
    n_slots = 4
    in_specs = [pl.BlockSpec(memory_space=pltpu.VMEM)] * (1 + len(groups))
    in_specs += [pl.BlockSpec(memory_space=pl.ANY)] * len(after)
    args = [std_a, *groups, *after]
    aliases = {}
    if buffer is not None:
        aliases = {len(args): 0}
        in_specs.append(pl.BlockSpec(memory_space=pl.ANY))
        args.append(buffer)
    return pl.pallas_call(
        functools.partial(product_kernel, len(groups), column),
        out_shape=jax.ShapeDtypeStruct((height, full_width), jnp.float32),
        in_specs=in_specs,
        out_specs=pl.BlockSpec(memory_space=pl.ANY),
        scratch_shapes=[
            pltpu.VMEM((n_slots, height, strip), jnp.float32),
            pltpu.SemaphoreType.DMA((n_slots, height // block_of(height, 1024))),
        ],
        input_output_aliases=aliases,
        compiler_params=pltpu.CompilerParams(vmem_limit_bytes=VMEM),
        cost_estimate=pl.CostEstimate(
            flops=2 * height * width * total, bytes_accessed=4 * height * width, transcendentals=0
        ),
        name="product_chunk",
    )(*args)


def sent(x, axis, step):
    size = lax.axis_size(axis)
    return lax.ppermute(x, axis, [(i, partner(i, step, size)) for i in range(size)])


def forwarded(block, axis, step, blocks, after=()):
    low = step & -step
    if power_of_two(lax.axis_size(axis)):
        held = blocks[step - low]
        return sent(stacked([held], after) if after else held, axis, low)
    return sent(block, axis, step)


def per_device(a_acts, b_acts):
    n_fa = lax.axis_size("fa")
    n_fb = lax.axis_size("fb")
    panels_a = cut_panels(a_acts, "fa")
    panels_b = cut_panels(b_acts, "fb")
    order = [0, 1, *reversed(range(2, n_fa))]
    own_a = [sent(panels_a[s], "fa", s) if s else panels_a[0] for s in order]
    own_b = [panels_b[0]] + [sent(panels_b[s], "fb", s) for s in range(1, n_fb)]
    width_a, full_width = panels_a[0].shape[1], panels_b[0].shape[1]
    widths = chunk_widths(full_width, (1, 1))
    stacks = [(own_a, [width_a], 0), (own_b, widths, 0), (own_b, [full_width], 0)]
    group_a, *parts_b, group_b = join_rows(stacks)

    def forward(groups, hold):
        for step in range(3, n_fa):
            if power_of_two(step):
                groups.append(sent(groups[0], "fa", step))
            else:
                groups.append(forwarded(groups[0], "fa", step, groups, hold if step == 3 else ()))

    first = parts_b[0]
    whole = sent(group_b, "fa", 1)
    chunks = [[first, None, sent(first, "fa", 2)]]
    all_a = [group_a]
    for step in range(1, n_fb):
        if power_of_two(step):
            all_a.append(sent(group_a, "fb", step))
        else:
            all_a.append(forwarded(group_a, "fb", step, all_a, chunks[0][2:3]))
    std_a = standardize_a(all_a, n_fa, n_fb)
    for part in parts_b[1:]:
        across = sent(stacked([part], chunks[-1][2:3]), "fa", 2)
        chunks.append([part, None, across])
    for groups, near in zip(chunks, join_rows([([whole], widths, 0)])):
        groups[1] = near
    forward(chunks[0], ())
    for groups in chunks[1:]:
        forward(groups, [std_a])

    buffer = None
    column = 0
    for place, groups in enumerate(chunks):
        after = [later[2] for later in chunks[place + 1 : place + 2]]
        ordered = [groups[s] for s in order]
        buffer = product_chunk(std_a, ordered, column, full_width, buffer, after)
        column += groups[0].shape[1]
    return buffer


def solution(mesh):
    placed = (P(("layers", "fa", "fb"), None), P(("layers", "fa", "fb"), None))
    return jax.shard_map(
        per_device, mesh=mesh, in_specs=placed, out_specs=P(("layers", "fa"), "fb"), check_vma=False
    )
```

```python
import functools

import jax
import jax.numpy as jnp
from jax import lax
from jax.experimental import pallas as pl
from jax.experimental.pallas import tpu as pltpu
from jax.sharding import PartitionSpec as P

EPS = 1e-05
VMEM = 48 * 1024 * 1024


def block_of(size, limit):
    tiles = size // 128
    best = 1
    for count in range(1, tiles + 1):
        if tiles % count == 0 and count * 128 <= limit:
            best = count
    return best * 128


def chunk_widths(width, shares):
    unit = 256 if width % 256 == 0 else 128
    tiles = width // unit
    ends = [round(tiles * sum(shares[: k + 1]) / sum(shares)) for k in range(len(shares))]
    counts = [end - start for start, end in zip([0] + ends, ends)]
    return [count * unit for count in counts if count > 0]


def over_count(values, count):
    if power_of_two(count):
        return values * (1.0 / count)
    return values / count


def standardize(values):
    count = values.shape[0]
    mean = over_count(jnp.sum(values, axis=0, keepdims=True), count)
    centred = values - mean
    var = over_count(jnp.sum(centred * centred, axis=0, keepdims=True), count)
    return (centred * lax.rsqrt(var + EPS)).astype(jnp.bfloat16)


def power_of_two(count):
    return count & (count - 1) == 0


def partner(place, step, size):
    if power_of_two(size):
        return place ^ step
    return (place + step) % size


def cut_kernel(axis, size, ref, *refs):
    outs, sems = refs[:-1], refs[-1]
    width = ref.shape[1] // size
    place = lax.axis_index(axis)
    started = []
    for step in range(size):
        start = pl.multiple_of(partner(place, step, size) * width, 128)
        copy = pltpu.make_async_copy(ref.at[:, pl.ds(start, width)], outs[step], sems.at[step])
        copy.start()
        started.append(copy)
    for copy in started:
        copy.wait()


def cut_panels(acts, axis):
    size = lax.axis_size(axis)
    tok, width = acts.shape
    return pl.pallas_call(
        functools.partial(cut_kernel, axis, size),
        out_shape=[jax.ShapeDtypeStruct((tok, width // size), acts.dtype)] * size,
        in_specs=[pl.BlockSpec(memory_space=pl.ANY)],
        out_specs=[pl.BlockSpec(memory_space=pltpu.VMEM)] * size,
        scratch_shapes=[pltpu.SemaphoreType.DMA((size,))],
        compiler_params=pltpu.CompilerParams(vmem_limit_bytes=VMEM),
        name="cut_panels",
    )(acts)


def join_kernel(shapes, *refs):
    n_in = sum(len_in for len_in, _, _ in shapes)
    n_out = sum(len_out for _, len_out, _ in shapes)
    ins, outs = refs[:n_in], refs[-n_out:]
    for len_in, len_out, column in shapes:
        tok = ins[0].shape[0]
        for out in outs[:len_out]:
            width = out.shape[1]
            for i in range(len_in):
                out[pl.ds(i * tok, tok), :] = ins[i][:, pl.ds(column, width)]
            column += width
        ins, outs = ins[len_in:], outs[len_out:]


def join_rows(groups, after=(), first=None):
    pieces = [piece for group, _, _ in groups for piece in group]
    order = list(range(len(pieces)))
    if first is not None:
        order.insert(0, order.pop(first))
    shapes = [
        jax.ShapeDtypeStruct((group[0].shape[0] * len(group), width), group[0].dtype)
        for group, widths, _ in groups
        for width in widths
    ]
    counts = [(len(group), len(widths), column) for group, widths, column in groups]

    def kernel(*refs):
        ins = [refs[order.index(place)] for place in range(len(pieces))]
        join_kernel(counts, *ins, *refs[len(pieces) :])

    return pl.pallas_call(
        kernel,
        out_shape=shapes,
        in_specs=[pl.BlockSpec(memory_space=pltpu.VMEM)] * len(pieces)
        + [pl.BlockSpec(memory_space=pl.ANY)] * len(after),
        out_specs=[pl.BlockSpec(memory_space=pltpu.VMEM)] * len(shapes),
        compiler_params=pltpu.CompilerParams(vmem_limit_bytes=VMEM),
        name="join_rows",
    )(*[pieces[place] for place in order], *after)


def stacked(pieces, after=()):
    return join_rows([(pieces, [pieces[0].shape[1]], 0)], after)[0]


def standardize_a_kernel(n_fa, n_fb, *refs):
    groups, out = refs[:n_fb], refs[-1]
    tok = groups[0].shape[0] // n_fa
    pieces = [
        group[pl.ds(i * tok, tok), :].astype(jnp.float32) for i in range(n_fa) for group in groups
    ]
    out[...] = standardize(jnp.concatenate(pieces, axis=0)).T


def standardize_a(groups, n_fa, n_fb):
    rows, width = groups[0].shape
    block = block_of(width, 512)
    total = rows * n_fb
    return pl.pallas_call(
        functools.partial(standardize_a_kernel, n_fa, n_fb),
        out_shape=jax.ShapeDtypeStruct((width, total), jnp.bfloat16),
        grid=(width // block,),
        in_specs=[pl.BlockSpec((rows, block), lambda i: (0, i))] * n_fb,
        out_specs=pl.BlockSpec((block, total), lambda i: (i, 0)),
        compiler_params=pltpu.CompilerParams(vmem_limit_bytes=VMEM),
        cost_estimate=pl.CostEstimate(
            flops=10 * width * total, bytes_accessed=4 * width * total, transcendentals=0
        ),
        name="standardize_a",
    )(*groups)


def product_kernel(n_groups, column, a_ref, *refs):
    groups = refs[:n_groups]
    out, slots, sems = refs[-3:]
    total, width = a_ref.shape[1], groups[0].shape[1]
    n_slots, height, strip = slots.shape

    def copy_of(step):
        slot = lax.rem(step, n_slots)
        place = pl.multiple_of(column + step * strip, 128)
        return pltpu.make_async_copy(slots.at[slot], out.at[:, pl.ds(place, strip)], sems.at[slot])

    @pl.loop(0, width // strip)
    def _(step):
        @pl.when(step >= n_slots)
        def _():
            copy_of(step - n_slots).wait()

        parts = []
        for part in range(strip // 128):
            columns = pl.ds(pl.multiple_of(step * strip + part * 128, 128), 128)
            pieces = [ref[:, columns].astype(jnp.float32) for ref in groups]
            parts.append(standardize(jnp.concatenate(pieces, axis=0)))
        std = jnp.concatenate(parts, axis=1)
        product = jnp.dot(a_ref[...], std, preferred_element_type=jnp.float32)
        slots[lax.rem(step, n_slots)] = over_count(product, total)
        copy_of(step).start()

    @pl.loop(max(width // strip - n_slots, 0), width // strip)
    def _(step):
        copy_of(step).wait()


def product_chunk(std_a, groups, column, full_width, buffer, after=()):
    height, total = std_a.shape
    width = groups[0].shape[1]
    strip = 256 if width % 256 == 0 else 128
    n_slots = 4
    in_specs = [pl.BlockSpec(memory_space=pltpu.VMEM)] * (1 + len(groups))
    in_specs += [pl.BlockSpec(memory_space=pl.ANY)] * len(after)
    args = [std_a, *groups, *after]
    aliases = {}
    if buffer is not None:
        aliases = {len(args): 0}
        in_specs.append(pl.BlockSpec(memory_space=pl.ANY))
        args.append(buffer)
    return pl.pallas_call(
        functools.partial(product_kernel, len(groups), column),
        out_shape=jax.ShapeDtypeStruct((height, full_width), jnp.float32),
        in_specs=in_specs,
        out_specs=pl.BlockSpec(memory_space=pl.ANY),
        scratch_shapes=[
            pltpu.VMEM((n_slots, height, strip), jnp.float32),
            pltpu.SemaphoreType.DMA((n_slots,)),
        ],
        input_output_aliases=aliases,
        compiler_params=pltpu.CompilerParams(vmem_limit_bytes=VMEM),
        cost_estimate=pl.CostEstimate(
            flops=2 * height * width * total, bytes_accessed=4 * height * width, transcendentals=0
        ),
        name="product_chunk",
    )(*args)


def sent(x, axis, step):
    size = lax.axis_size(axis)
    return lax.ppermute(x, axis, [(i, partner(i, step, size)) for i in range(size)])


def forwarded(block, axis, step, blocks, after=()):
    low = step & -step
    if power_of_two(lax.axis_size(axis)):
        held = blocks[step - low]
        return sent(stacked([held], after) if after else held, axis, low)
    return sent(block, axis, step)


def per_device(a_acts, b_acts):
    n_fa = lax.axis_size("fa")
    n_fb = lax.axis_size("fb")
    panels_a = cut_panels(a_acts, "fa")
    panels_b = cut_panels(b_acts, "fb")
    order = [0, 1, *reversed(range(2, n_fa))]
    own_a = [sent(panels_a[s], "fa", s) if s else panels_a[0] for s in order]
    own_b = [panels_b[0]] + [sent(panels_b[s], "fb", s) for s in range(1, n_fb)]
    width_a, full_width = panels_a[0].shape[1], panels_b[0].shape[1]
    widths = chunk_widths(full_width, (1, 1))
    stacks = [(own_a, [width_a], 0), (own_b, widths, 0), (own_b, [full_width], 0)]
    group_a, *parts_b, group_b = join_rows(stacks)

    def forward(groups, hold):
        for step in range(3, n_fa):
            if power_of_two(step):
                groups.append(sent(groups[0], "fa", step))
            else:
                groups.append(forwarded(groups[0], "fa", step, groups, hold if step == 3 else ()))

    first = parts_b[0]
    whole = sent(group_b, "fa", 1)
    chunks = [[first, None, sent(first, "fa", 2)]]
    all_a = [group_a]
    for step in range(1, n_fb):
        if power_of_two(step):
            all_a.append(sent(group_a, "fb", step))
        else:
            all_a.append(forwarded(group_a, "fb", step, all_a, chunks[0][2:3]))
    std_a = standardize_a(all_a, n_fa, n_fb)
    for part in parts_b[1:]:
        across = sent(stacked([part], chunks[-1][2:3]), "fa", 2)
        chunks.append([part, None, across])
    for groups, near in zip(chunks, join_rows([([whole], widths, 0)])):
        groups[1] = near
    forward(chunks[0], ())
    for groups in chunks[1:]:
        forward(groups, [std_a])

    buffer = None
    column = 0
    for place, groups in enumerate(chunks):
        after = [later[2] for later in chunks[place + 1 : place + 2]]
        ordered = [groups[s] for s in order]
        buffer = product_chunk(std_a, ordered, column, full_width, buffer, after)
        column += groups[0].shape[1]
    return buffer


def solution(mesh):
    placed = (P(("layers", "fa", "fb"), None), P(("layers", "fa", "fb"), None))
    return jax.shard_map(
        per_device, mesh=mesh, in_specs=placed, out_specs=P(("layers", "fa"), "fb"), check_vma=False
    )
```

```python
import functools

import jax
import jax.numpy as jnp
from jax import lax
from jax.experimental import pallas as pl
from jax.experimental.pallas import tpu as pltpu
from jax.sharding import PartitionSpec as P

EPS = 1e-05
VMEM = 48 * 1024 * 1024


def block_of(size, limit):
    tiles = size // 128
    best = 1
    for count in range(1, tiles + 1):
        if tiles % count == 0 and count * 128 <= limit:
            best = count
    return best * 128


def chunk_widths(width, shares):
    unit = 256 if width % 256 == 0 else 128
    tiles = width // unit
    ends = [round(tiles * sum(shares[: k + 1]) / sum(shares)) for k in range(len(shares))]
    counts = [end - start for start, end in zip([0] + ends, ends)]
    return [count * unit for count in counts if count > 0]


def over_count(values, count):
    if power_of_two(count):
        return values * (1.0 / count)
    return values / count


def standardize(values):
    count = values.shape[0]
    mean = over_count(jnp.sum(values, axis=0, keepdims=True), count)
    centred = values - mean
    var = over_count(jnp.sum(centred * centred, axis=0, keepdims=True), count)
    return (centred * lax.rsqrt(var + EPS)).astype(jnp.bfloat16)


def power_of_two(count):
    return count & (count - 1) == 0


def partner(place, step, size):
    if power_of_two(size):
        return place ^ step
    return (place + step) % size


def cut_kernel(axis, size, ref, *refs):
    outs, sems = refs[:-1], refs[-1]
    width = ref.shape[1] // size
    place = lax.axis_index(axis)
    started = []
    for step in range(size):
        start = pl.multiple_of(partner(place, step, size) * width, 128)
        copy = pltpu.make_async_copy(ref.at[:, pl.ds(start, width)], outs[step], sems.at[step])
        copy.start()
        started.append(copy)
    for copy in started:
        copy.wait()


def cut_panels(acts, axis):
    size = lax.axis_size(axis)
    tok, width = acts.shape
    return pl.pallas_call(
        functools.partial(cut_kernel, axis, size),
        out_shape=[jax.ShapeDtypeStruct((tok, width // size), acts.dtype)] * size,
        in_specs=[pl.BlockSpec(memory_space=pl.ANY)],
        out_specs=[pl.BlockSpec(memory_space=pltpu.VMEM)] * size,
        scratch_shapes=[pltpu.SemaphoreType.DMA((size,))],
        compiler_params=pltpu.CompilerParams(vmem_limit_bytes=VMEM),
        name="cut_panels",
    )(acts)


def join_kernel(shapes, *refs):
    n_in = sum(len_in for len_in, _, _ in shapes)
    n_out = sum(len_out for _, len_out, _ in shapes)
    ins, outs = refs[:n_in], refs[-n_out:]
    for len_in, len_out, column in shapes:
        tok = ins[0].shape[0]
        for out in outs[:len_out]:
            width = out.shape[1]
            for i in range(len_in):
                out[pl.ds(i * tok, tok), :] = ins[i][:, pl.ds(column, width)]
            column += width
        ins, outs = ins[len_in:], outs[len_out:]


def join_rows(groups, after=(), first=None):
    pieces = [piece for group, _, _ in groups for piece in group]
    order = list(range(len(pieces)))
    if first is not None:
        order.insert(0, order.pop(first))
    shapes = [
        jax.ShapeDtypeStruct((group[0].shape[0] * len(group), width), group[0].dtype)
        for group, widths, _ in groups
        for width in widths
    ]
    counts = [(len(group), len(widths), column) for group, widths, column in groups]

    def kernel(*refs):
        ins = [refs[order.index(place)] for place in range(len(pieces))]
        join_kernel(counts, *ins, *refs[len(pieces) :])

    return pl.pallas_call(
        kernel,
        out_shape=shapes,
        in_specs=[pl.BlockSpec(memory_space=pltpu.VMEM)] * len(pieces)
        + [pl.BlockSpec(memory_space=pl.ANY)] * len(after),
        out_specs=[pl.BlockSpec(memory_space=pltpu.VMEM)] * len(shapes),
        compiler_params=pltpu.CompilerParams(vmem_limit_bytes=VMEM),
        name="join_rows",
    )(*[pieces[place] for place in order], *after)


def stacked(pieces, after=()):
    return join_rows([(pieces, [pieces[0].shape[1]], 0)], after)[0]


def standardize_a_kernel(n_fa, n_fb, *refs):
    groups, out = refs[:n_fb], refs[-1]
    tok = groups[0].shape[0] // n_fa
    pieces = [
        group[pl.ds(i * tok, tok), :].astype(jnp.float32) for i in range(n_fa) for group in groups
    ]
    out[...] = standardize(jnp.concatenate(pieces, axis=0)).T


def standardize_a(groups, n_fa, n_fb):
    rows, width = groups[0].shape
    block = block_of(width, 512)
    total = rows * n_fb
    return pl.pallas_call(
        functools.partial(standardize_a_kernel, n_fa, n_fb),
        out_shape=jax.ShapeDtypeStruct((width, total), jnp.bfloat16),
        grid=(width // block,),
        in_specs=[pl.BlockSpec((rows, block), lambda i: (0, i))] * n_fb,
        out_specs=pl.BlockSpec((block, total), lambda i: (i, 0)),
        compiler_params=pltpu.CompilerParams(vmem_limit_bytes=VMEM),
        cost_estimate=pl.CostEstimate(
            flops=10 * width * total, bytes_accessed=4 * width * total, transcendentals=0
        ),
        name="standardize_a",
    )(*groups)


def product_kernel(n_groups, column, a_ref, *refs):
    groups = refs[:n_groups]
    out, slots, edges, sems, edge_sems = refs[-5:]
    total, width = a_ref.shape[1], groups[0].shape[1]
    n_slots, height, strip = slots.shape
    edge = edges.shape[2]
    steps = (width - 2 * edge) // strip

    def product_of(start, size):
        parts = []
        for part in range(size // 128):
            columns = pl.ds(pl.multiple_of(start + part * 128, 128), 128)
            pieces = [ref[:, columns].astype(jnp.float32) for ref in groups]
            parts.append(standardize(jnp.concatenate(pieces, axis=0)))
        std = parts[0] if len(parts) == 1 else jnp.concatenate(parts, axis=1)
        product = jnp.dot(a_ref[...], std, preferred_element_type=jnp.float32)
        return over_count(product, total)

    def copy_of(step):
        slot = lax.rem(step, n_slots)
        place = pl.multiple_of(column + edge + step * strip, 128)
        return pltpu.make_async_copy(slots.at[slot], out.at[:, pl.ds(place, strip)], sems.at[slot])

    def edge_copy(side):
        place = column + side * (width - edge)
        return pltpu.make_async_copy(edges.at[side], out.at[:, pl.ds(place, edge)], edge_sems.at[side])

    edges[0] = product_of(0, edge)
    edge_copy(0).start()

    @pl.loop(0, steps)
    def _(step):
        @pl.when(step >= n_slots)
        def _():
            copy_of(step - n_slots).wait()

        slots[lax.rem(step, n_slots)] = product_of(edge + step * strip, strip)
        copy_of(step).start()

    edges[1] = product_of(width - edge, edge)
    edge_copy(1).start()

    @pl.loop(max(steps - n_slots, 0), steps)
    def _(step):
        copy_of(step).wait()

    edge_copy(0).wait()
    edge_copy(1).wait()


def product_chunk(std_a, groups, column, full_width, buffer, after=()):
    height, total = std_a.shape
    width = groups[0].shape[1]
    strip = 256 if width % 256 == 0 else 128
    n_slots = 4
    in_specs = [pl.BlockSpec(memory_space=pltpu.VMEM)] * (1 + len(groups))
    in_specs += [pl.BlockSpec(memory_space=pl.ANY)] * len(after)
    args = [std_a, *groups, *after]
    aliases = {}
    if buffer is not None:
        aliases = {len(args): 0}
        in_specs.append(pl.BlockSpec(memory_space=pl.ANY))
        args.append(buffer)
    return pl.pallas_call(
        functools.partial(product_kernel, len(groups), column),
        out_shape=jax.ShapeDtypeStruct((height, full_width), jnp.float32),
        in_specs=in_specs,
        out_specs=pl.BlockSpec(memory_space=pl.ANY),
        scratch_shapes=[
            pltpu.VMEM((n_slots, height, strip), jnp.float32),
            pltpu.VMEM((2, height, 128), jnp.float32),
            pltpu.SemaphoreType.DMA((n_slots,)),
            pltpu.SemaphoreType.DMA((2,)),
        ],
        input_output_aliases=aliases,
        compiler_params=pltpu.CompilerParams(vmem_limit_bytes=VMEM),
        cost_estimate=pl.CostEstimate(
            flops=2 * height * width * total, bytes_accessed=4 * height * width, transcendentals=0
        ),
        name="product_chunk",
    )(*args)


def sent(x, axis, step):
    size = lax.axis_size(axis)
    return lax.ppermute(x, axis, [(i, partner(i, step, size)) for i in range(size)])


def forwarded(block, axis, step, blocks, after=()):
    low = step & -step
    if power_of_two(lax.axis_size(axis)):
        held = blocks[step - low]
        return sent(stacked([held], after) if after else held, axis, low)
    return sent(block, axis, step)


def per_device(a_acts, b_acts):
    n_fa = lax.axis_size("fa")
    n_fb = lax.axis_size("fb")
    panels_a = cut_panels(a_acts, "fa")
    panels_b = cut_panels(b_acts, "fb")
    order = [0, 1, *reversed(range(2, n_fa))]
    own_a = [sent(panels_a[s], "fa", s) if s else panels_a[0] for s in order]
    own_b = [panels_b[0]] + [sent(panels_b[s], "fb", s) for s in range(1, n_fb)]
    width_a, full_width = panels_a[0].shape[1], panels_b[0].shape[1]
    widths = chunk_widths(full_width, (1, 1))
    stacks = [(own_a, [width_a], 0), (own_b, widths, 0), (own_b, [full_width], 0)]
    group_a, *parts_b, group_b = join_rows(stacks)

    def forward(groups, hold):
        for step in range(3, n_fa):
            if power_of_two(step):
                groups.append(sent(groups[0], "fa", step))
            else:
                groups.append(forwarded(groups[0], "fa", step, groups, hold if step == 3 else ()))

    first = parts_b[0]
    whole = sent(group_b, "fa", 1)
    chunks = [[first, None, sent(first, "fa", 2)]]
    all_a = [group_a]
    for step in range(1, n_fb):
        if power_of_two(step):
            all_a.append(sent(group_a, "fb", step))
        else:
            all_a.append(forwarded(group_a, "fb", step, all_a, chunks[0][2:3]))
    std_a = standardize_a(all_a, n_fa, n_fb)
    for part in parts_b[1:]:
        across = sent(stacked([part], chunks[-1][2:3]), "fa", 2)
        chunks.append([part, None, across])
    for groups, near in zip(chunks, join_rows([([whole], widths, 0)])):
        groups[1] = near
    forward(chunks[0], ())
    for groups in chunks[1:]:
        forward(groups, [std_a])

    buffer = None
    column = 0
    for place, groups in enumerate(chunks):
        after = [later[2] for later in chunks[place + 1 : place + 2]]
        ordered = [groups[s] for s in order]
        buffer = product_chunk(std_a, ordered, column, full_width, buffer, after)
        column += groups[0].shape[1]
    return buffer


def solution(mesh):
    placed = (P(("layers", "fa", "fb"), None), P(("layers", "fa", "fb"), None))
    return jax.shard_map(
        per_device, mesh=mesh, in_specs=placed, out_specs=P(("layers", "fa"), "fb"), check_vma=False
    )
```

```python
import functools

import jax
import jax.numpy as jnp
from jax import lax
from jax.experimental import pallas as pl
from jax.experimental.pallas import tpu as pltpu
from jax.sharding import PartitionSpec as P

EPS = 1e-05
VMEM = 48 * 1024 * 1024


def block_of(size, limit):
    tiles = size // 128
    best = 1
    for count in range(1, tiles + 1):
        if tiles % count == 0 and count * 128 <= limit:
            best = count
    return best * 128


def chunk_widths(width, shares):
    unit = 256 if width % 256 == 0 else 128
    tiles = width // unit
    ends = [round(tiles * sum(shares[: k + 1]) / sum(shares)) for k in range(len(shares))]
    counts = [end - start for start, end in zip([0] + ends, ends)]
    return [count * unit for count in counts if count > 0]


def over_count(values, count):
    if power_of_two(count):
        return values * (1.0 / count)
    return values / count


def standardize(values, scale=1.0):
    count = values.shape[0]
    mean = over_count(jnp.sum(values, axis=0, keepdims=True), count)
    centred = values - mean
    var = over_count(jnp.sum(centred * centred, axis=0, keepdims=True), count)
    return (centred * (lax.rsqrt(var + EPS) * scale)).astype(jnp.bfloat16)


def power_of_two(count):
    return count & (count - 1) == 0


def partner(place, step, size):
    if power_of_two(size):
        return place ^ step
    return (place + step) % size


def cut_kernel(axis, size, ref, *refs):
    outs, sems = refs[:-1], refs[-1]
    width = ref.shape[1] // size
    place = lax.axis_index(axis)
    started = []
    for step in range(size):
        start = pl.multiple_of(partner(place, step, size) * width, 128)
        copy = pltpu.make_async_copy(ref.at[:, pl.ds(start, width)], outs[step], sems.at[step])
        copy.start()
        started.append(copy)
    for copy in started:
        copy.wait()


def cut_panels(acts, axis):
    size = lax.axis_size(axis)
    tok, width = acts.shape
    return pl.pallas_call(
        functools.partial(cut_kernel, axis, size),
        out_shape=[jax.ShapeDtypeStruct((tok, width // size), acts.dtype)] * size,
        in_specs=[pl.BlockSpec(memory_space=pl.ANY)],
        out_specs=[pl.BlockSpec(memory_space=pltpu.VMEM)] * size,
        scratch_shapes=[pltpu.SemaphoreType.DMA((size,))],
        compiler_params=pltpu.CompilerParams(vmem_limit_bytes=VMEM),
        name="cut_panels",
    )(acts)


def join_kernel(shapes, *refs):
    n_in = sum(len_in for len_in, _, _ in shapes)
    n_out = sum(len_out for _, len_out, _ in shapes)
    ins, outs = refs[:n_in], refs[-n_out:]
    for len_in, len_out, column in shapes:
        tok = ins[0].shape[0]
        for out in outs[:len_out]:
            width = out.shape[1]
            for i in range(len_in):
                out[pl.ds(i * tok, tok), :] = ins[i][:, pl.ds(column, width)]
            column += width
        ins, outs = ins[len_in:], outs[len_out:]


def join_rows(groups, after=(), first=None):
    pieces = [piece for group, _, _ in groups for piece in group]
    order = list(range(len(pieces)))
    if first is not None:
        order.insert(0, order.pop(first))
    shapes = [
        jax.ShapeDtypeStruct((group[0].shape[0] * len(group), width), group[0].dtype)
        for group, widths, _ in groups
        for width in widths
    ]
    counts = [(len(group), len(widths), column) for group, widths, column in groups]

    def kernel(*refs):
        ins = [refs[order.index(place)] for place in range(len(pieces))]
        join_kernel(counts, *ins, *refs[len(pieces) :])

    return pl.pallas_call(
        kernel,
        out_shape=shapes,
        in_specs=[pl.BlockSpec(memory_space=pltpu.VMEM)] * len(pieces)
        + [pl.BlockSpec(memory_space=pl.ANY)] * len(after),
        out_specs=[pl.BlockSpec(memory_space=pltpu.VMEM)] * len(shapes),
        compiler_params=pltpu.CompilerParams(vmem_limit_bytes=VMEM),
        name="join_rows",
    )(*[pieces[place] for place in order], *after)


def stacked(pieces, after=()):
    return join_rows([(pieces, [pieces[0].shape[1]], 0)], after)[0]


def standardize_a_kernel(n_fa, n_fb, *refs):
    groups, out = refs[:n_fb], refs[-1]
    tok = groups[0].shape[0] // n_fa
    pieces = [
        group[pl.ds(i * tok, tok), :].astype(jnp.float32) for i in range(n_fa) for group in groups
    ]
    values = jnp.concatenate(pieces, axis=0)
    total = values.shape[0]
    out[...] = standardize(values, 1.0 / total if power_of_two(total) else 1.0).T


def standardize_a(groups, n_fa, n_fb):
    rows, width = groups[0].shape
    block = block_of(width, 512)
    total = rows * n_fb
    return pl.pallas_call(
        functools.partial(standardize_a_kernel, n_fa, n_fb),
        out_shape=jax.ShapeDtypeStruct((width, total), jnp.bfloat16),
        grid=(width // block,),
        in_specs=[pl.BlockSpec((rows, block), lambda i: (0, i))] * n_fb,
        out_specs=pl.BlockSpec((block, total), lambda i: (i, 0)),
        compiler_params=pltpu.CompilerParams(vmem_limit_bytes=VMEM),
        cost_estimate=pl.CostEstimate(
            flops=10 * width * total, bytes_accessed=4 * width * total, transcendentals=0
        ),
        name="standardize_a",
    )(*groups)


def product_kernel(n_groups, column, a_ref, *refs):
    groups = refs[:n_groups]
    out, slots, sems = refs[-3:]
    total, width = a_ref.shape[1], groups[0].shape[1]
    n_slots, height, strip = slots.shape

    def copy_of(step):
        slot = lax.rem(step, n_slots)
        place = pl.multiple_of(column + step * strip, 128)
        return pltpu.make_async_copy(slots.at[slot], out.at[:, pl.ds(place, strip)], sems.at[slot])

    @pl.loop(0, width // strip)
    def _(step):
        @pl.when(step >= n_slots)
        def _():
            copy_of(step - n_slots).wait()

        parts = []
        for part in range(strip // 128):
            columns = pl.ds(pl.multiple_of(step * strip + part * 128, 128), 128)
            pieces = [ref[:, columns].astype(jnp.float32) for ref in groups]
            parts.append(standardize(jnp.concatenate(pieces, axis=0)))
        std = jnp.concatenate(parts, axis=1)
        product = jnp.dot(a_ref[...], std, preferred_element_type=jnp.float32)
        slots[lax.rem(step, n_slots)] = product if power_of_two(total) else product / total
        copy_of(step).start()

    @pl.loop(max(width // strip - n_slots, 0), width // strip)
    def _(step):
        copy_of(step).wait()


def product_chunk(std_a, groups, column, full_width, buffer, after=()):
    height, total = std_a.shape
    width = groups[0].shape[1]
    strip = 256 if width % 256 == 0 else 128
    n_slots = 4
    in_specs = [pl.BlockSpec(memory_space=pltpu.VMEM)] * (1 + len(groups))
    in_specs += [pl.BlockSpec(memory_space=pl.ANY)] * len(after)
    args = [std_a, *groups, *after]
    aliases = {}
    if buffer is not None:
        aliases = {len(args): 0}
        in_specs.append(pl.BlockSpec(memory_space=pl.ANY))
        args.append(buffer)
    return pl.pallas_call(
        functools.partial(product_kernel, len(groups), column),
        out_shape=jax.ShapeDtypeStruct((height, full_width), jnp.float32),
        in_specs=in_specs,
        out_specs=pl.BlockSpec(memory_space=pl.ANY),
        scratch_shapes=[
            pltpu.VMEM((n_slots, height, strip), jnp.float32),
            pltpu.SemaphoreType.DMA((n_slots,)),
        ],
        input_output_aliases=aliases,
        compiler_params=pltpu.CompilerParams(vmem_limit_bytes=VMEM),
        cost_estimate=pl.CostEstimate(
            flops=2 * height * width * total, bytes_accessed=4 * height * width, transcendentals=0
        ),
        name="product_chunk",
    )(*args)


def sent(x, axis, step):
    size = lax.axis_size(axis)
    return lax.ppermute(x, axis, [(i, partner(i, step, size)) for i in range(size)])


def forwarded(block, axis, step, blocks, after=()):
    low = step & -step
    if power_of_two(lax.axis_size(axis)):
        held = blocks[step - low]
        return sent(stacked([held], after) if after else held, axis, low)
    return sent(block, axis, step)


def per_device(a_acts, b_acts):
    n_fa = lax.axis_size("fa")
    n_fb = lax.axis_size("fb")
    panels_a = cut_panels(a_acts, "fa")
    panels_b = cut_panels(b_acts, "fb")
    order = [0, 1, *reversed(range(2, n_fa))]
    own_a = [sent(panels_a[s], "fa", s) if s else panels_a[0] for s in order]
    own_b = [panels_b[0]] + [sent(panels_b[s], "fb", s) for s in range(1, n_fb)]
    width_a, full_width = panels_a[0].shape[1], panels_b[0].shape[1]
    widths = chunk_widths(full_width, (1, 1))
    stacks = [(own_a, [width_a], 0), (own_b, widths, 0), (own_b, [full_width], 0)]
    group_a, *parts_b, group_b = join_rows(stacks)

    def forward(groups, hold):
        for step in range(3, n_fa):
            if power_of_two(step):
                groups.append(sent(groups[0], "fa", step))
            else:
                groups.append(forwarded(groups[0], "fa", step, groups, hold if step == 3 else ()))

    first = parts_b[0]
    whole = sent(group_b, "fa", 1)
    chunks = [[first, None, sent(first, "fa", 2)]]
    all_a = [group_a]
    for step in range(1, n_fb):
        if power_of_two(step):
            all_a.append(sent(group_a, "fb", step))
        else:
            all_a.append(forwarded(group_a, "fb", step, all_a, chunks[0][2:3]))
    std_a = standardize_a(all_a, n_fa, n_fb)
    for part in parts_b[1:]:
        across = sent(stacked([part], chunks[-1][2:3]), "fa", 2)
        chunks.append([part, None, across])
    for groups, near in zip(chunks, join_rows([([whole], widths, 0)])):
        groups[1] = near
    forward(chunks[0], ())
    for groups in chunks[1:]:
        forward(groups, [std_a])

    buffer = None
    column = 0
    for place, groups in enumerate(chunks):
        after = [later[2] for later in chunks[place + 1 : place + 2]]
        ordered = [groups[s] for s in order]
        buffer = product_chunk(std_a, ordered, column, full_width, buffer, after)
        column += groups[0].shape[1]
    return buffer


def solution(mesh):
    placed = (P(("layers", "fa", "fb"), None), P(("layers", "fa", "fb"), None))
    return jax.shard_map(
        per_device, mesh=mesh, in_specs=placed, out_specs=P(("layers", "fa"), "fb"), check_vma=False
    )
```
